32 devices in a mesh: blk: 8 (over y, x, core), group: 4 (over z).
Axes of the slice: x: 2, y: 2, z: 4, core: 2. Of those that a mesh axis runs over, the one named last changes fastest.
Arguments:
- codes: bfloat16 [16384, 1024], P(('blk', 'group')), may hold values from -6 to 6
- row_scale: bfloat16 [16384], P(('blk', 'group')), may hold values from 0.3 to 3
- row_group: int32 [16384, 1], P(('blk', 'group')), may hold values from 0 to 3; in each aligned block of 512 rows (0 to 511, 512 to 1023, ...) at most 192 rows name the same one
- row_sub: int32 [16384], P(('blk', 'group')), may hold values from 0 to 1
- centroids: bfloat16 [8, 1024], P('group'), may hold values from -6 to 6
Outputs:
- best_sim: float32 [16384], P(('blk', 'group'))
The draws below stay inside these ranges and needn't reach their ends.
Inputs may be any that keep to these rules, and one draw needn't show every extreme that they name: `row_group`: among the rows of one device no cluster group is named by more than 192 rows, and in every draw some device has a group named by exactly 192 of its rows.
All inputs are finite; a program needn't handle non-finite values.
Results may differ from the reference program's by a relative error of at most 0.0003.
Values may be sent and summed in bfloat16 or wider, within the bound.
No kernel may reach another device: no remote copies, remote signals or barrier semaphores. Data moves between devices by JAX's collectives and lax.ppermute only.
A program may use at most 128 MiB of HBM per device.

```python
import math
import jax
import jax.numpy as jnp
import numpy as np
from jax import lax

D = 1024
ROW_DEV = 512
CL_GROUP = 2
CAP = 192
ROWS = 16384
CLUSTERS = 8
N_GROUP = 4


def copy_anchor(key):
    positions = jnp.arange(ROWS, dtype=jnp.int32)
    picked = jax.random.randint(jax.random.fold_in(key, 101), (ROWS,), 0, 2)
    source = jax.random.randint(jax.random.fold_in(key, 102), (ROWS,), 0, jnp.maximum(positions, 1))
    copied = (picked == 1) & (positions > 0)
    source_free = jnp.logical_not(copied[source])
    return jnp.where(copied & source_free, source, positions).astype(jnp.int32)


def draw_codes(key, part):
    anchor = copy_anchor(key)
    key = jax.random.fold_in(key, 3)
    base = jnp.clip(jax.random.normal(key, (ROWS, D), jnp.float32), -6.0, 6.0)
    return base[anchor].astype(jnp.bfloat16)


def draw_row_scale(key, part):
    anchor = copy_anchor(key)
    key = jax.random.fold_in(key, 5)
    base = jnp.exp(jax.random.uniform(key, (ROWS,), jnp.float32, jnp.log(0.3), jnp.log(3.0)))
    return base[anchor].astype(jnp.bfloat16)


def with_ends(result, rng, low, top_value):
    extent = result.shape
    index_at = [jax.random.randint(jax.random.fold_in(rng, axis), (), 0, extent[axis]) for axis in range(len(extent))]
    result = result.at[tuple(index_at)].set(low)
    longest = extent.index(max(extent))
    index_at[longest] = (index_at[longest] + 1) % extent[longest]
    return result.at[tuple(index_at)].set(top_value)


def shard_levels(key, extent, split, least, high):
    def one(dim, parts):
        heights = jax.random.uniform(jax.random.fold_in(jax.random.fold_in(key, 6), dim), (parts,), jnp.float32, least / len(split), high / len(split))
        return jnp.repeat(jnp.exp(heights), extent[dim] // parts).reshape((-1,) + (1,) * (len(extent) - dim - 1))

    factor_of = one(*split[0])
    for cut in split[1:]:
        factor_of = factor_of * one(*cut)
    return factor_of


def shared_out(key, own, number, rows, number_of, top, bound, slope):
    ranking = jax.random.permutation(key, number_of)
    heavy_load, common = load_shares(number_of, rows * top, bound, slope, True), load_shares(number_of, rows * top, bound, slope, False)
    places = jnp.arange(number_of)

    def named(sizes, rotation):
        used = int((sizes > 0).sum())
        fixed = max(1, used // 4)
        moved = fixed + (places - fixed + rotation * (used - fixed)) % max(1, number_of - fixed)
        return jnp.zeros((number_of,), jnp.int32).at[ranking[jnp.where(places < fixed, places, moved)]].set(jnp.asarray(sizes, jnp.int32))

    sizes = jnp.where(number % 4 == 0, named(heavy_load, number // 4), named(common, number - number // 4 - 1))
    mixed = jax.random.permutation(jax.random.fold_in(own, 3), number_of)
    donor, receiver = mixed[0:number_of // 2 * 2:2], mixed[1:number_of // 2 * 2:2]
    margin = jnp.minimum(sizes[donor] - 1, bound - sizes[receiver]) // 2
    margin = jnp.where((donor == ranking[0]) | (receiver == ranking[0]) | (sizes[receiver] == 0), 0, jnp.maximum(margin, 0))
    moved = jax.random.randint(jax.random.fold_in(own, 4), (number_of // 2,), 0, 1 << 20) % (margin + 1)
    sizes = sizes.at[donor].add(-moved).at[receiver].add(moved)
    labels = jnp.searchsorted(jnp.cumsum(sizes), jnp.arange(rows * top), side="right").astype(jnp.int32)
    grid = labels.reshape(top, rows).T
    grid = grid[jax.random.permutation(jax.random.fold_in(own, 1), rows)]
    rotation = jax.random.randint(jax.random.fold_in(own, 2), (rows, 1), 0, top)
    return jnp.take_along_axis(grid, (jnp.arange(top)[None, :] + rotation) % top, axis=1)


def load_shares(amount, total, most, slope, full):
    portions = [(1 << 20) // math.isqrt(rank ** slope) + 1 for rank in range(1, amount + 1)]
    largest = most if full else min(most, max(-(-total // amount), total * portions[0] // sum(portions)))
    least = 1 if total - largest >= amount - 1 else 0
    counts, rest = [largest] + [least] * (amount - 1), total - largest - least * (amount - 1)
    while rest > 0:
        free = [i for i in range(1, amount) if counts[i] < largest] or [i for i in range(1, amount) if counts[i] < most]
        whole, remaining = sum([portions[i] for i in free]), rest
        for i in free:
            more = min(most - counts[i], max(1, remaining * portions[i] // whole), rest)
            counts[i] = counts[i] + more
            rest = rest - more
    return np.array(counts)


def gaussian(own_key, dims, width, bound, pieces=(), held_as=jnp.bfloat16):
    entries = jax.random.normal(own_key, dims, jnp.float32) * width
    if len(pieces) > 0:
        entries = shard_levels(own_key, dims, pieces, -0.22, 0.18) * entries
    return jnp.clip(entries, min=-bound, max=bound).astype(held_as)


def setup_inputs(seed: int = 0) -> dict:
    arg_keys = jax.random.split(jax.random.key(seed), 6)
    codes = draw_codes(jax.random.fold_in(arg_keys[5], 71), 0)
    row_scale = draw_row_scale(jax.random.fold_in(arg_keys[5], 71), 0)
    row_group_keys = jax.random.split(jax.random.fold_in(arg_keys[2], 1), ROWS // ROW_DEV)
    row_group_turns = jax.random.permutation(jax.random.fold_in(arg_keys[2], 3), ROWS // ROW_DEV)
    row_group = jax.vmap(lambda own, number: shared_out(jax.random.fold_in(arg_keys[2], 2), own, number, ROW_DEV, N_GROUP, 1, CAP, 2))(row_group_keys, row_group_turns).reshape((ROWS, 1))
    row_sub = with_ends(jax.random.randint(arg_keys[3], (ROWS,), 0, CL_GROUP), jax.random.fold_in(arg_keys[3], 1), 0, CL_GROUP - 1).astype(jnp.int32)
    centroids = gaussian(arg_keys[4], (CLUSTERS, D), 1.0, 6.0, ((0, 4),))
    return dict(codes=codes, row_scale=row_scale, row_group=row_group, row_sub=row_sub, centroids=centroids)


def scored(best_sim, query_rows, query_clus, query_order, key_rows, key_clus, key_order):
    scores = jnp.einsum('qd,kd->qk', query_rows.astype(jnp.float32), key_rows.astype(jnp.float32))
    allowed = (key_clus[None, :] == query_clus[:, None]) & (key_order[None, :] < query_order[:, None]) & (key_order[None, :] > 0)
    return jnp.maximum(best_sim, lax.optimization_barrier(jnp.max(jnp.where(allowed, scores, -1.0), axis=1)))

def reference(codes, row_scale, row_group, row_sub, centroids):
    cluster = (row_group[:, 0] * CL_GROUP + row_sub).astype(jnp.int32)
    vectors = centroids[cluster].astype(jnp.float32) + row_scale.astype(jnp.float32)[:, None] * codes.astype(jnp.float32)
    unit_rows = (vectors / jnp.sqrt(lax.optimization_barrier(jnp.sum(vectors * vectors, axis=1, keepdims=True)) + 1e-06)).astype(jnp.bfloat16)
    row_total = cluster.shape[0]
    sorter = jnp.argsort(cluster, stable=True).astype(jnp.int32)
    sorted_rows = unit_rows[sorter]
    sorted_clus = cluster[sorter]
    sorted_order = (sorter + 1).astype(jnp.int32)
    positions = jnp.arange(row_total, dtype=jnp.int32)
    firsts = jnp.concatenate([jnp.ones((1,), dtype=bool), sorted_clus[1:] != sorted_clus[:-1]])
    cluster_start = lax.cummax(jnp.where(firsts, positions, 0).astype(jnp.int32), axis=0)
    block_len = 512 if row_total % 512 == 0 else row_total

    def one_block(block_no):
        first_row = (block_no * block_len).astype(jnp.int32)
        query_rows = lax.dynamic_slice_in_dim(sorted_rows, first_row, block_len)
        query_clus = lax.dynamic_slice_in_dim(sorted_clus, first_row, block_len)
        query_order = lax.dynamic_slice_in_dim(sorted_order, first_row, block_len)
        low_start = (cluster_start[first_row] // block_len * block_len).astype(jnp.int32)
        steps_needed = ((first_row - low_start) // block_len + 1).astype(jnp.int32)

        def visit_keys(stride, best_sim):
            key_start = (low_start + stride * block_len).astype(jnp.int32)
            key_rows = lax.dynamic_slice_in_dim(sorted_rows, key_start, block_len)
            key_clus = lax.dynamic_slice_in_dim(sorted_clus, key_start, block_len)
            key_order = lax.dynamic_slice_in_dim(sorted_order, key_start, block_len)
            return scored(best_sim, query_rows, query_clus, query_order, key_rows, key_clus, key_order)
        start_sim = jnp.full((block_len,), -1.0, dtype=jnp.float32)
        return lax.fori_loop(jnp.int32(0), steps_needed, visit_keys, start_sim)
    best_sorted = lax.map(one_block, jnp.arange(row_total // block_len, dtype=jnp.int32))
    return jnp.zeros((row_total,), dtype=jnp.float32).at[sorter].set(best_sorted.reshape(-1))
```

```python
import functools

import jax
import jax.numpy as jnp
from jax import lax
from jax.experimental import pallas as pl
from jax.experimental.pallas import tpu as pltpu
from jax.sharding import PartitionSpec as P

META = 16
OWN, SIB, XN, YN = 0, 1, 2, 3
VMEM_LIMIT = 48 * 1024 * 1024


def dot_last(a, b):
    return lax.dot_general(a, b, (((1,), (1,)), ((), ())), preferred_element_type=jnp.float32)


def as_column(row):
    n = row.shape[1]
    eye = lax.broadcasted_iota(jnp.int32, (n, n), 0) == lax.broadcasted_iota(jnp.int32, (n, n), 1)
    return jnp.sum(jnp.where(eye, row, 0.0), axis=1, keepdims=True)


def vmem_specs(count):
    return [pl.BlockSpec(memory_space=pltpu.VMEM)] * count


def pack_kernel(cap, groups, aux_ref, codes_ref, *out_refs):
    chunk_refs, place_ref = out_refs[:groups], out_refs[groups]
    rows = codes_ref.shape[0]
    group_pos = lax.axis_index("group")
    hop = aux_ref[2:3, :].astype(jnp.int32) ^ group_pos
    member = (lax.broadcasted_iota(jnp.int32, (16, rows), 0) == hop).astype(jnp.bfloat16)
    upto = (
        lax.broadcasted_iota(jnp.int32, (rows, rows), 0)
        <= lax.broadcasted_iota(jnp.int32, (rows, rows), 1)
    ).astype(jnp.bfloat16)
    counts = jnp.dot(member, upto, preferred_element_type=jnp.float32)
    rank = jnp.sum(counts * member.astype(jnp.float32), axis=0, keepdims=True).astype(jnp.int32) - 1
    place_ref[...] = jnp.concatenate([hop, rank] + [jnp.zeros_like(rank)] * 6, axis=0)
    meta_rows = jnp.concatenate(
        [aux_ref[0:2, :], jnp.zeros((META - 2, rows), jnp.float32)], axis=0
    ).astype(jnp.bfloat16)
    codes = codes_ref[...]
    slots = lax.broadcasted_iota(jnp.int32, (cap, rows), 0)
    for s in range(groups):
        pick = (slots == jnp.where(hop == s, rank, -1)).astype(jnp.bfloat16)
        chunk_refs[s][0:cap, :] = jnp.dot(pick, codes, preferred_element_type=jnp.float32).astype(
            jnp.bfloat16
        )
        chunk_refs[s][cap:, :] = jnp.zeros((META, codes.shape[1]), jnp.bfloat16)
        chunk_refs[s][cap:, 0:cap] = dot_last(meta_rows, pick).astype(jnp.bfloat16)


def unit_kernel(cap, chunk_ref, cent_ref, out_ref):
    meta = chunk_ref[cap:, 0:cap].astype(jnp.float32)
    scale = as_column(meta[0:1, :])
    code = as_column(meta[1:2, :])
    cent = cent_ref[...].astype(jnp.float32)
    centre = jnp.where(code == 2.0, cent[1:2, :], cent[0:1, :])
    vectors = centre + scale * chunk_ref[0:cap, :].astype(jnp.float32)
    norm = jnp.sqrt(jnp.sum(vectors * vectors, axis=1, keepdims=True) + 1e-06)
    out_ref[0:cap, :] = (vectors * (1.0 / norm)).astype(jnp.bfloat16)
    out_ref[cap:, :] = chunk_ref[cap:, :]


def score_kernel(cap, old, new, *refs):
    chunks = old + new
    count = len(chunks)
    ins = refs[: 4 * count]
    before = refs[4 * count : 4 * count + 3] if old else ()
    own_ref, x_ref, y_ref, data, meta, acc, sem = refs[4 * count + len(before) :]
    blk = lax.axis_index("blk")
    group_pos = lax.axis_index("group")
    core, x, y = blk % 2, (blk // 2) % 2, blk // 4
    copies = []
    for block in range(4):
        for at in range(count):
            source = ins[block * count + at]
            copies.append(
                (
                    pltpu.make_async_copy(
                        source.at[0:cap, :],
                        data.at[block, at * cap : (at + 1) * cap, :],
                        sem.at[0, block, at],
                    ),
                    pltpu.make_async_copy(
                        source.at[cap:, 0:256], meta.at[block, at], sem.at[1, block, at]
                    ),
                )
            )
    for pair in copies:
        pair[0].start()
        pair[1].start()
    acc[...] = jnp.full(acc.shape, -1.0, jnp.float32)
    if old:
        for block, ref in zip((OWN, XN, YN), before):
            acc[block, 0:4, :] = ref[...]
    for pair in copies:
        pair[0].wait()
        pair[1].wait()

    def codes_of(block, at):
        return meta[block, at][1:2, 0:cap].astype(jnp.float32)

    def score(early, late, late_at, early_from, early_to, own_pair=False):
        e_rows = data[early, early_from * cap : early_to * cap, :]
        l_rows = data[late, late_at * cap : (late_at + 1) * cap, :]
        scores = dot_last(e_rows, l_rows)
        l_code = codes_of(late, late_at)
        best = acc[late, chunks[late_at] : chunks[late_at] + 1, :]
        for at in range(early_from, early_to):
            part = scores[(at - early_from) * cap : (at - early_from + 1) * cap, :]
            allowed = as_column(codes_of(early, at)) == l_code
            if own_pair:
                if at == late_at:
                    allowed &= lax.broadcasted_iota(
                        jnp.int32, (cap, cap), 0
                    ) < lax.broadcasted_iota(jnp.int32, (cap, cap), 1)
                else:
                    limit = jnp.where(
                        (group_pos ^ chunks[at]) < (group_pos ^ chunks[late_at]), cap, 0
                    )
                    allowed &= lax.broadcasted_iota(jnp.int32, (cap, cap), 0) < limit
            best = jnp.maximum(
                best, jnp.max(jnp.where(allowed, part, -1.0), axis=0, keepdims=True)
            )
        acc[late, chunks[late_at] : chunks[late_at] + 1, :] = best

    def all_of(early, late, own_pair=False):
        for late_at in range(count):
            if late_at < len(old):
                score(early, late, late_at, len(old), count, own_pair)
            else:
                score(early, late, late_at, 0, count, own_pair)

    def one_pair(number, carry):
        late = jnp.where(
            number == 0,
            jnp.where(x == 0, XN, OWN),
            jnp.where(
                number == 1,
                jnp.where(y == 0, YN, OWN),
                jnp.where(number == 2, jnp.where(y == 0, YN, XN), OWN),
            ),
        )
        both = jnp.where(
            number == 0,
            OWN + XN,
            jnp.where(number == 1, OWN + YN, jnp.where(number == 2, XN + YN, OWN + SIB)),
        )
        all_of(both - late, late)
        return carry

    all_of(OWN, OWN, own_pair=True)
    lax.fori_loop(0, 3 + core, one_pair, 0)
    own_ref[...] = acc[OWN, 0:4, :]
    x_ref[...] = acc[XN, 0:4, :]
    y_ref[...] = acc[YN, 0:4, :]


def restore_kernel(cap, groups, place_ref, *refs):
    parts, out_ref = refs[:groups], refs[groups]
    rows = place_ref.shape[1]
    hop, rank = place_ref[0:1, :], place_ref[1:2, :]
    slots = lax.broadcasted_iota(jnp.int32, (cap, rows), 0)
    total = jnp.zeros((16, rows), jnp.float32)
    for s in range(groups):
        value = parts[s][...]
        high = value.astype(jnp.bfloat16)
        rest = value - high.astype(jnp.float32)
        middle = rest.astype(jnp.bfloat16)
        low = (rest - middle.astype(jnp.float32)).astype(jnp.bfloat16)
        stacked = jnp.concatenate(
            [high.astype(jnp.float32), middle.astype(jnp.float32), low.astype(jnp.float32)]
            + [jnp.zeros((13, cap), jnp.float32)],
            axis=0,
        ).astype(jnp.bfloat16)
        pick = (slots == jnp.where(hop == s, rank, -1)).astype(jnp.bfloat16)
        total = total + jnp.dot(stacked, pick, preferred_element_type=jnp.float32)
    out_ref[...] = total[0:1, :] + (total[1:2, :] + total[2:3, :])


def blk_of(y, x, core):
    return (y * 2 + x) * 2 + core


def plane_pairs():
    to_x, to_y, to_sib = [], [], []
    for y in range(2):
        for x in range(2):
            for core in range(2):
                me = blk_of(y, x, core)
                to_x.append((blk_of(y, 1 - x, core ^ x ^ y), me))
                to_y.append((blk_of(1 - y, x, core ^ y), me))

            to_sib.append((blk_of(y, x, 0), blk_of(y, x, 1)))
    return to_x, to_y, to_sib


def reverse(pairs):
    return [(b, a) for a, b in pairs]


def score_call(cap, old, new, blocks, before, width):
    count = len(old) + len(new)
    arrays = [block[at] for block in blocks for at in old + new]
    shape = jax.ShapeDtypeStruct((4, cap), jnp.float32)
    pairs = 5 * (count * count - len(old) ** 2)
    return pl.pallas_call(
        functools.partial(score_kernel, cap, tuple(old), tuple(new)),
        out_shape=[shape] * 3,
        in_specs=[pl.BlockSpec(memory_space=pl.ANY)] * (4 * count) + vmem_specs(len(before)),
        out_specs=vmem_specs(3),
        scratch_shapes=[
            pltpu.VMEM((4, count * cap, width), jnp.bfloat16),
            pltpu.VMEM((4, count, META, 256), jnp.bfloat16),
            pltpu.VMEM((4, 8, cap), jnp.float32),
            pltpu.SemaphoreType.DMA((2, 4, count)),
        ],
        compiler_params=pltpu.CompilerParams(vmem_limit_bytes=VMEM_LIMIT),
        cost_estimate=pl.CostEstimate(
            flops=2 * pairs * cap * cap * width,
            bytes_accessed=8 * count * cap * width,
            transcendentals=0,
        ),
    )(*arrays, *before)


def paired_shards(codes, row_scale, row_group, row_sub, centroids):
    row_count, width = codes.shape
    groups = lax.axis_size("group")
    cap = 3 * row_count // (2 * groups)
    params = pltpu.CompilerParams(vmem_limit_bytes=VMEM_LIMIT)
    aux = jnp.stack(
        [
            row_scale.astype(jnp.float32),
            row_sub.astype(jnp.float32) + 1.0,
            row_group[:, 0].astype(jnp.float32),
            jnp.zeros((row_count,), jnp.float32),
        ]
    )
    chunk_shape = jax.ShapeDtypeStruct((cap + META, width), jnp.bfloat16)
    *packed, place = pl.pallas_call(
        functools.partial(pack_kernel, cap, groups),
        out_shape=[chunk_shape] * groups + [jax.ShapeDtypeStruct((8, row_count), jnp.int32)],
        in_specs=vmem_specs(2),
        out_specs=vmem_specs(groups + 1),
        compiler_params=params,
    )(aux, codes)
    hops = [[(g, g ^ s) for g in range(groups)] for s in range(groups)]
    arrived = [None] * groups
    for s in (2, 3, 1):
        arrived[s] = lax.ppermute(packed[s], "group", hops[s])
    arrived[0] = packed[0]
    unit_call = pl.pallas_call(
        functools.partial(unit_kernel, cap),
        out_shape=chunk_shape,
        in_specs=vmem_specs(2),
        out_specs=pl.BlockSpec(memory_space=pltpu.VMEM),
        compiler_params=params,
        cost_estimate=pl.CostEstimate(
            flops=8 * cap * width, bytes_accessed=4 * cap * width, transcendentals=0
        ),
    )
    to_x, to_y, to_sib = plane_pairs()
    blocks = [[None] * groups for _ in range(4)]
    for s in (0, 1, 2, 3):
        unit = unit_call(arrived[s], centroids)
        blocks[OWN][s] = unit
        blocks[XN][s] = lax.ppermute(unit, "blk", to_x)
        blocks[YN][s] = lax.ppermute(unit, "blk", to_y)
        blocks[SIB][s] = lax.ppermute(unit, "blk", to_sib)
    before = score_call(cap, [], [0, 1, 2], blocks, [], width)
    best, for_x, for_y = score_call(cap, [0, 1, 2], [3], blocks, before, width)
    best = jnp.maximum(
        best,
        jnp.maximum(
            lax.ppermute(for_x, "blk", reverse(to_x)), lax.ppermute(for_y, "blk", reverse(to_y))
        ),
    )
    returned = [best[0:1]] + [
        lax.ppermute(best[s : s + 1], "group", hops[s]) for s in range(1, groups)
    ]
    out = pl.pallas_call(
        functools.partial(restore_kernel, cap, groups),
        out_shape=jax.ShapeDtypeStruct((1, row_count), jnp.float32),
        in_specs=vmem_specs(groups + 1),
        out_specs=pl.BlockSpec(memory_space=pltpu.VMEM),
        compiler_params=params,
    )(place, *returned)
    return out.reshape(row_count)


def compare(best_sim, own_rows, own_order, own_sub, key_rows, key_order, key_sub):
    scores = jnp.einsum("qd,kd->qk", own_rows, key_rows, preferred_element_type=jnp.float32)
    allowed = (
        (key_sub[None, :] == own_sub[:, None])
        & (key_order[None, :] < own_order[:, None])
        & (key_order[None, :] > 0)
    )
    return jnp.maximum(best_sim, jnp.max(jnp.where(allowed, scores, -1.0), axis=1))


def gathered_shards(codes, row_scale, row_group, row_sub, centroids):
    row_count, width = codes.shape
    groups = lax.axis_size("group")
    capacity = 3 * row_count // (2 * groups)
    slot_count = groups * capacity
    cycle_pos = lax.axis_index("blk")
    group_pos = lax.axis_index("group")
    target = row_group[:, 0]
    member = (target[:, None] == jnp.arange(groups, dtype=jnp.int32)[None, :]).astype(jnp.int32)
    slot_rank = jnp.sum((jnp.cumsum(member, axis=0) - 1) * member, axis=1)
    placed = target * capacity + slot_rank
    row_order = (
        (cycle_pos * groups + group_pos) * row_count + jnp.arange(row_count, dtype=jnp.int32) + 1
    )

    def send(values):
        slots = jnp.zeros((slot_count,) + values.shape[1:], values.dtype).at[placed].set(values)
        return lax.all_to_all(
            slots.reshape((groups, capacity) + values.shape[1:]), "group", 0, 0, tiled=True
        )

    part_codes, part_scale = send(codes), send(row_scale)
    part_sub, part_order = send(row_sub), send(row_order)
    picks = (part_sub[..., None] == jnp.arange(centroids.shape[0], dtype=jnp.int32)).astype(
        jnp.bfloat16
    )
    centre = jnp.einsum("gnc,cd->gnd", picks, centroids, preferred_element_type=jnp.float32)
    vectors = centre + part_scale.astype(jnp.float32)[..., None] * part_codes.astype(jnp.float32)
    unit_part = (
        vectors / jnp.sqrt(jnp.sum(vectors * vectors, axis=-1, keepdims=True) + 1e-06)
    ).astype(jnp.bfloat16)
    own_rows = unit_part.reshape(slot_count, width)
    own_order = part_order.reshape(slot_count)
    own_sub = part_sub.reshape(slot_count)
    stacked = tuple(lax.all_gather(a, "blk", axis=0) for a in (own_rows, own_order, own_sub))

    def per_shard(carry, item):
        return compare(carry, own_rows, own_order, own_sub, *item), None

    start_sim = jnp.full((slot_count,), -1.0, jnp.float32)
    best_sim = lax.scan(per_shard, start_sim, stacked)[0]
    returned = lax.all_to_all(best_sim.reshape(groups, capacity), "group", 0, 0, tiled=True)
    return returned.reshape(-1)[placed]


def solution(mesh):
    paired = mesh.shape["blk"] == 8 and mesh.shape["group"] == 4
    return jax.shard_map(
        paired_shards if paired else gathered_shards,
        mesh=mesh,
        in_specs=(
            P(("blk", "group"), None),
            P(("blk", "group")),
            P(("blk", "group"), None),
            P(("blk", "group")),
            P("group", None),
        ),
        out_specs=P(("blk", "group")),
        check_vma=False,
    )
```

```python
import functools

import jax
import jax.numpy as jnp
from jax import lax
from jax.experimental import pallas as pl
from jax.experimental.pallas import tpu as pltpu
from jax.sharding import PartitionSpec as P

META = 8
OWN, SIB, XN, YN = 0, 1, 2, 3
VMEM_LIMIT = 20 * 1024 * 1024


def dot_last(a, b):
    return lax.dot_general(a, b, (((1,), (1,)), ((), ())), preferred_element_type=jnp.float32)


def iota(shape, dim):
    return lax.broadcasted_iota(jnp.int32, shape, dim)


def as_column(row):
    n = row.shape[1]
    return jnp.sum(jnp.where(iota((n, n), 0) == iota((n, n), 1), row, 0.0), axis=1, keepdims=True)


def vmem_specs(count):
    return [pl.BlockSpec(memory_space=pltpu.VMEM)] * count


def pack_kernel(cap, groups, group_ref, sub_ref, scale_ref, codes_ref, *out_refs):
    chunk_refs, place_ref = out_refs[:groups], out_refs[groups]
    rows, width = codes_ref.shape
    hop = group_ref[...] ^ lax.axis_index("group")
    keys = iota((16, rows), 0)
    member = keys == hop * 2 + sub_ref[...]
    upto = (iota((rows, rows), 0) <= iota((rows, rows), 1)).astype(jnp.bfloat16)
    counts = jnp.dot(member.astype(jnp.bfloat16), upto, preferred_element_type=jnp.float32)
    totals = counts[:, rows - 1 : rows]
    before = jnp.concatenate([jnp.zeros((1, 1), jnp.float32), totals[:-1]], axis=0)
    base = jnp.where(keys % 2 == 1, before, 0.0) - 1.0
    rank = jnp.sum(jnp.where(member, counts + base, 0.0), axis=0, keepdims=True).astype(jnp.int32)
    place_ref[...] = jnp.concatenate([hop, rank] + [jnp.zeros_like(rank)] * 6, axis=0)
    scales = jnp.concatenate(
        [scale_ref[...], jnp.zeros((15, rows), jnp.float32)], axis=0
    ).astype(jnp.bfloat16)
    codes = codes_ref[...]
    for s in range(groups):
        pick = (iota((cap, rows), 0) == jnp.where(hop == s, rank, -1)).astype(jnp.bfloat16)
        chunk_refs[s][0:cap, :] = jnp.dot(pick, codes, preferred_element_type=jnp.float32).astype(
            jnp.bfloat16
        )
        first = jnp.broadcast_to(totals[2 * s : 2 * s + 1, :], (1, cap))
        both = first + totals[2 * s + 1 : 2 * s + 2, :]
        meta = jnp.concatenate(
            [dot_last(scales, pick)[0:1, :], first, both, jnp.zeros((META - 3, cap), jnp.float32)],
            axis=0,
        )
        chunk_refs[s][cap:, :] = jnp.concatenate(
            [meta, jnp.zeros((META, width - cap), jnp.float32)], axis=1
        ).astype(jnp.bfloat16)


def unit_kernel(cap, chunk_ref, cent_ref, out_ref):
    meta = chunk_ref[cap:, 0:cap].astype(jnp.float32)
    scale = as_column(meta[0:1, :])
    first = meta[1:2, 0:1].astype(jnp.int32)
    cent = cent_ref[...].astype(jnp.float32)
    centre = jnp.where(iota((cap, 1), 0) < first, cent[0:1, :], cent[1:2, :])
    vectors = centre + scale * chunk_ref[0:cap, :].astype(jnp.float32)
    norm = jnp.sqrt(jnp.sum(vectors * vectors, axis=1, keepdims=True) + 1e-06)
    out_ref[0:cap, :] = (vectors * (1.0 / norm)).astype(jnp.bfloat16)
    out_ref[cap:, :] = chunk_ref[cap:, :]


def score_kernel(cap, old, new, *refs):
    chunks = old + new
    count = len(chunks)
    data = [dict(zip(chunks, refs[block * count : (block + 1) * count])) for block in range(4)]
    rest = refs[4 * count :]
    best_refs = dict(zip((OWN, XN, YN), rest[-3:]))
    blk = lax.axis_index("blk")
    group_pos = lax.axis_index("group")
    core, x, y = blk % 2, (blk // 2) % 2, blk // 4
    row = iota((cap, cap), 0)
    lane = iota((1, cap), 1)
    if old:
        for block, ref in zip((OWN, XN, YN), rest[:3]):
            best_refs[block][...] = ref[...]
    else:
        for block in (OWN, XN, YN):
            best_refs[block][...] = jnp.full((4, cap), -1.0, jnp.float32)

    def sizes(block, at):
        meta = data[block][at][cap:, 0:cap].astype(jnp.float32).astype(jnp.int32)
        return meta[1:2, :], meta[2:3, :]

    def score(early, late):
        for late_at in chunks:
            late_first = lane < sizes(late, late_at)[0]
            best = best_refs[late][late_at : late_at + 1, :]
            for at in chunks if late_at in new else new:
                scores = dot_last(data[early][at][0:cap, :], data[late][late_at][0:cap, :])
                first, both = sizes(early, at)
                low = jnp.where(late_first, 0, first)
                high = jnp.where(late_first, first, both)
                if early == late:
                    if at == late_at:
                        high = jnp.minimum(high, lane)
                    else:
                        high = jnp.where((group_pos ^ at) < (group_pos ^ late_at), high, 0)
                kept = jnp.where((row >= low) & (row < high), scores, -1.0)
                best = jnp.maximum(best, jnp.max(kept, axis=0, keepdims=True))
            best_refs[late][late_at : late_at + 1, :] = best

    score(OWN, OWN)
    pl.when(x == 0)(lambda: score(OWN, XN))
    pl.when(x == 1)(lambda: score(XN, OWN))

    @pl.when(y == 0)
    def _():
        score(OWN, YN)
        score(XN, YN)

    @pl.when(y == 1)
    def _():
        score(YN, OWN)
        score(YN, XN)

    pl.when(core == 1)(lambda: score(SIB, OWN))


def split_kernel(own_ref, x_ref, y_ref, *out_refs):
    best = jnp.maximum(own_ref[...], jnp.maximum(x_ref[...], y_ref[...]))
    for s, ref in enumerate(out_refs):
        ref[...] = best[s : s + 1, :]


def restore_kernel(cap, groups, place_ref, *refs):
    parts, out_ref = refs[:groups], refs[groups]
    rows = place_ref.shape[1]
    hop, rank = place_ref[0:1, :], place_ref[1:2, :]
    total = jnp.zeros((16, rows), jnp.float32)
    for s in range(groups):
        value = parts[s][...]
        high = value.astype(jnp.bfloat16)
        rest = value - high.astype(jnp.float32)
        middle = rest.astype(jnp.bfloat16)
        low = rest - middle.astype(jnp.float32)
        stacked = jnp.concatenate(
            [high.astype(jnp.float32), middle.astype(jnp.float32), low]
            + [jnp.zeros((13, cap), jnp.float32)],
            axis=0,
        ).astype(jnp.bfloat16)
        pick = (iota((cap, rows), 0) == jnp.where(hop == s, rank, -1)).astype(jnp.bfloat16)
        total = total + jnp.dot(stacked, pick, preferred_element_type=jnp.float32)
    out_ref[...] = total[0:1, :] + (total[1:2, :] + total[2:3, :])


def blk_of(y, x, core):
    return (y * 2 + x) * 2 + core


def plane_pairs():
    to_x, to_y, to_sib = [], [], []
    for y in range(2):
        for x in range(2):
            for core in range(2):
                me = blk_of(y, x, core)
                to_x.append((blk_of(y, 1 - x, core ^ x ^ y), me))
                to_y.append((blk_of(1 - y, x, core ^ y), me))
            to_sib.append((blk_of(y, x, 0), blk_of(y, x, 1)))
    return to_x, to_y, to_sib


def reverse(pairs):
    return [(b, a) for a, b in pairs]


def after(value, *others):
    return lax.optimization_barrier((value,) + others)[0]


def score_call(cap, old, new, blocks, before, width):
    count = len(old) + len(new)
    arrays = [block[at] for block in blocks for at in old + new]
    pairs = 5 * (count * count - len(old) ** 2)
    return pl.pallas_call(
        functools.partial(score_kernel, cap, tuple(old), tuple(new)),
        out_shape=[jax.ShapeDtypeStruct((4, cap), jnp.float32)] * 3,
        in_specs=vmem_specs(4 * count + len(before)),
        out_specs=vmem_specs(3),
        compiler_params=pltpu.CompilerParams(vmem_limit_bytes=VMEM_LIMIT),
        cost_estimate=pl.CostEstimate(
            flops=2 * pairs * cap * cap * width,
            bytes_accessed=8 * count * cap * width,
            transcendentals=0,
        ),
    )(*arrays, *before)


def paired_shards(codes, row_scale, row_group, row_sub, centroids):
    row_count, width = codes.shape
    groups = lax.axis_size("group")
    cap = 3 * row_count // (2 * groups)
    params = pltpu.CompilerParams(vmem_limit_bytes=VMEM_LIMIT)
    chunk_shape = jax.ShapeDtypeStruct((cap + META, width), jnp.bfloat16)
    *packed, place = pl.pallas_call(
        functools.partial(pack_kernel, cap, groups),
        out_shape=[chunk_shape] * groups + [jax.ShapeDtypeStruct((8, row_count), jnp.int32)],
        in_specs=vmem_specs(4),
        out_specs=vmem_specs(groups + 1),
        compiler_params=params,
    )(
        row_group.reshape(1, row_count),
        row_sub.reshape(1, row_count),
        row_scale.astype(jnp.float32).reshape(1, row_count),
        codes,
    )
    hops = [[(g, g ^ s) for g in range(groups)] for s in range(groups)]
    unit_call = pl.pallas_call(
        functools.partial(unit_kernel, cap),
        out_shape=chunk_shape,
        in_specs=vmem_specs(2),
        out_specs=pl.BlockSpec(memory_space=pltpu.VMEM),
        compiler_params=params,
        cost_estimate=pl.CostEstimate(
            flops=8 * cap * width, bytes_accessed=4 * cap * width, transcendentals=0
        ),
    )
    to_x, to_y, to_sib = plane_pairs()
    blocks = [[None] * groups for _ in range(4)]

    def spread(s, chunk, sib_after=(), x_after=(), y_after=()):
        unit = unit_call(chunk, centroids)
        blocks[OWN][s] = unit
        blocks[SIB][s] = lax.ppermute(after(unit, *sib_after), "blk", to_sib)
        blocks[XN][s] = lax.ppermute(after(unit, *x_after), "blk", to_x)
        blocks[YN][s] = lax.ppermute(after(unit, *y_after), "blk", to_y)

    one = lax.ppermute(packed[1], "group", hops[1])
    two = lax.ppermute(packed[2], "group", hops[2])
    three = lax.ppermute(after(packed[3], one), "group", hops[3])
    spread(0, packed[0])
    _, sib0, x0, y0 = (block[0] for block in blocks)
    spread(1, one, [sib0], [x0], [y0])
    best0 = score_call(cap, [], [0], blocks, [], width)
    _, sib1, x1, y1 = (block[1] for block in blocks)
    spread(2, after(two, sib1, *best0), [x1, y1])
    best1 = score_call(cap, [0], [1], blocks, best0, width)
    spread(3, after(three, blocks[SIB][2], *best1))
    best2 = score_call(cap, [0, 1], [2], blocks, best1, width)
    best, for_x, for_y = score_call(cap, [0, 1, 2], [3], blocks, best2, width)
    returned = pl.pallas_call(
        split_kernel,
        out_shape=[jax.ShapeDtypeStruct((1, cap), jnp.float32)] * groups,
        in_specs=vmem_specs(3),
        out_specs=vmem_specs(groups),
        compiler_params=params,
    )(best, lax.ppermute(for_x, "blk", reverse(to_x)), lax.ppermute(for_y, "blk", reverse(to_y)))
    returned = [returned[0]] + [
        lax.ppermute(returned[s], "group", hops[s]) for s in range(1, groups)
    ]
    out = pl.pallas_call(
        functools.partial(restore_kernel, cap, groups),
        out_shape=jax.ShapeDtypeStruct((1, row_count), jnp.float32),
        in_specs=vmem_specs(groups + 1),
        out_specs=pl.BlockSpec(memory_space=pltpu.VMEM),
        compiler_params=params,
    )(place, *returned)
    return out.reshape(row_count)


def compare(best_sim, own_rows, own_order, own_sub, key_rows, key_order, key_sub):
    scores = jnp.einsum("qd,kd->qk", own_rows, key_rows, preferred_element_type=jnp.float32)
    allowed = (
        (key_sub[None, :] == own_sub[:, None])
        & (key_order[None, :] < own_order[:, None])
        & (key_order[None, :] > 0)
    )
    return jnp.maximum(best_sim, jnp.max(jnp.where(allowed, scores, -1.0), axis=1))


def gathered_shards(codes, row_scale, row_group, row_sub, centroids):
    row_count, width = codes.shape
    groups = lax.axis_size("group")
    capacity = 3 * row_count // (2 * groups)
    slot_count = groups * capacity
    cycle_pos = lax.axis_index("blk")
    group_pos = lax.axis_index("group")
    target = row_group[:, 0]
    member = (target[:, None] == jnp.arange(groups, dtype=jnp.int32)[None, :]).astype(jnp.int32)
    slot_rank = jnp.sum((jnp.cumsum(member, axis=0) - 1) * member, axis=1)
    placed = target * capacity + slot_rank
    row_order = (
        (cycle_pos * groups + group_pos) * row_count + jnp.arange(row_count, dtype=jnp.int32) + 1
    )

    def send(values):
        slots = jnp.zeros((slot_count,) + values.shape[1:], values.dtype).at[placed].set(values)
        return lax.all_to_all(
            slots.reshape((groups, capacity) + values.shape[1:]), "group", 0, 0, tiled=True
        )

    part_codes, part_scale = send(codes), send(row_scale)
    part_sub, part_order = send(row_sub), send(row_order)
    picks = (part_sub[..., None] == jnp.arange(centroids.shape[0], dtype=jnp.int32)).astype(
        jnp.bfloat16
    )
    centre = jnp.einsum("gnc,cd->gnd", picks, centroids, preferred_element_type=jnp.float32)
    vectors = centre + part_scale.astype(jnp.float32)[..., None] * part_codes.astype(jnp.float32)
    unit_part = (
        vectors / jnp.sqrt(jnp.sum(vectors * vectors, axis=-1, keepdims=True) + 1e-06)
    ).astype(jnp.bfloat16)
    own_rows = unit_part.reshape(slot_count, width)
    own_order = part_order.reshape(slot_count)
    own_sub = part_sub.reshape(slot_count)
    stacked = tuple(lax.all_gather(a, "blk", axis=0) for a in (own_rows, own_order, own_sub))

    def per_shard(carry, item):
        return compare(carry, own_rows, own_order, own_sub, *item), None

    start_sim = jnp.full((slot_count,), -1.0, jnp.float32)
    best_sim = lax.scan(per_shard, start_sim, stacked)[0]
    returned = lax.all_to_all(best_sim.reshape(groups, capacity), "group", 0, 0, tiled=True)
    return returned.reshape(-1)[placed]


def solution(mesh):
    paired = mesh.shape["blk"] == 8 and mesh.shape["group"] == 4
    return jax.shard_map(
        paired_shards if paired else gathered_shards,
        mesh=mesh,
        in_specs=(
            P(("blk", "group"), None),
            P(("blk", "group")),
            P(("blk", "group"), None),
            P(("blk", "group")),
            P("group", None),
        ),
        out_specs=P(("blk", "group")),
        check_vma=False,
    )
```

```python
import functools

import jax
import jax.numpy as jnp
from jax import lax
from jax.experimental import pallas as pl
from jax.experimental.pallas import tpu as pltpu
from jax.sharding import PartitionSpec as P

META = 8
OWN, SIB, XN, YN = 0, 1, 2, 3
VMEM_LIMIT = 20 * 1024 * 1024
COST = pl.CostEstimate(flops=1, bytes_accessed=1, transcendentals=0)


def dot_last(a, b):
    return lax.dot_general(a, b, (((1,), (1,)), ((), ())), preferred_element_type=jnp.float32)


def iota(shape, dim):
    return lax.broadcasted_iota(jnp.int32, shape, dim)


def as_column(row):
    n = row.shape[1]
    return jnp.sum(jnp.where(iota((n, n), 0) == iota((n, n), 1), row, 0.0), axis=1, keepdims=True)


def vmem_specs(count):
    return [pl.BlockSpec(memory_space=pltpu.VMEM)] * count


def pack_kernel(cap, group_ref, sub_ref, scale_ref, codes_ref, *out_refs):
    chunk_refs, place_ref = out_refs[:-1], out_refs[-1]
    rows, width = codes_ref.shape
    hop = group_ref[...] ^ lax.axis_index("group")
    keys = iota((16, rows), 0)
    member = keys == hop * 2 + sub_ref[...]
    upto = (iota((rows, rows), 0) <= iota((rows, rows), 1)).astype(jnp.bfloat16)
    counts = jnp.dot(member.astype(jnp.bfloat16), upto, preferred_element_type=jnp.float32)
    totals = counts[:, rows - 1 : rows]
    before = jnp.concatenate([jnp.zeros((1, 1), jnp.float32), totals[:-1]], axis=0)
    base = jnp.where(keys % 2 == 1, before, 0.0) - 1.0
    rank = jnp.sum(jnp.where(member, counts + base, 0.0), axis=0, keepdims=True).astype(jnp.int32)
    place_ref[...] = jnp.concatenate([hop, rank] + [jnp.zeros_like(rank)] * 6, axis=0)
    scales = jnp.concatenate(
        [scale_ref[...], jnp.zeros((15, rows), jnp.float32)], axis=0
    ).astype(jnp.bfloat16)
    codes = codes_ref[...]
    for s, ref in enumerate(chunk_refs):
        pick = (iota((cap, rows), 0) == jnp.where(hop == s, rank, -1)).astype(jnp.bfloat16)
        ref[0:cap, :] = jnp.dot(pick, codes, preferred_element_type=jnp.float32).astype(
            jnp.bfloat16
        )
        first = jnp.broadcast_to(totals[2 * s : 2 * s + 1, :], (1, cap))
        both = first + totals[2 * s + 1 : 2 * s + 2, :]
        meta = jnp.concatenate(
            [dot_last(scales, pick)[0:1, :], first, both, jnp.zeros((META - 3, cap), jnp.float32)],
            axis=0,
        )
        ref[cap:, :] = jnp.concatenate(
            [meta, jnp.zeros((META, width - cap), jnp.float32)], axis=1
        ).astype(jnp.bfloat16)


def unit_kernel(cap, *refs):
    chunk_refs, cent_ref, out_ref = refs[:-2], refs[-2], refs[-1]
    count = len(chunk_refs)
    cent = cent_ref[...].astype(jnp.float32)
    for at, ref in enumerate(chunk_refs):
        meta = ref[cap:, 0:cap].astype(jnp.float32)
        scale = as_column(meta[0:1, :])
        first = meta[1:2, 0:1].astype(jnp.int32)
        centre = jnp.where(iota((cap, 1), 0) < first, cent[0:1, :], cent[1:2, :])
        vectors = centre + scale * ref[0:cap, :].astype(jnp.float32)
        norm = jnp.sqrt(jnp.sum(vectors * vectors, axis=1, keepdims=True) + 1e-06)
        out_ref[at * cap : (at + 1) * cap, :] = (vectors * (1.0 / norm)).astype(jnp.bfloat16)
        start = count * cap + at * META
        out_ref[start : start + META, :] = ref[cap:, :]


def blocks_used(inner, outer):
    return (OWN,) + (SIB,) * inner + (XN, YN) * outer


def score_kernel(cap, old, new, inner, outer, *refs):
    parts = old + new
    chunks = sum(parts, ())
    fresh = sum(new, ())
    used = blocks_used(inner, outer)
    arrays = {
        (block, part): refs[at * len(parts) + which]
        for at, block in enumerate(used)
        for which, part in enumerate(parts)
    }
    part_of = {chunk: part for part in parts for chunk in part}
    rest = refs[len(arrays) :]
    best_refs = dict(zip((OWN, XN, YN), rest[-3:]))
    blk = lax.axis_index("blk")
    group_pos = lax.axis_index("group")
    core, x, y = blk % 2, (blk // 2) % 2, blk // 4
    row, lane = iota((cap, cap), 0), iota((1, cap), 1)
    if len(rest) > 3:
        for block, ref in zip((OWN, XN, YN), rest[:3]):
            best_refs[block][...] = ref[...]
    else:
        for block in (OWN, XN, YN):
            best_refs[block][...] = jnp.full((4, cap), -1.0, jnp.float32)

    def rows_of(block, chunk):
        part = part_of[chunk]
        at = part.index(chunk)
        return arrays[block, part][at * cap : (at + 1) * cap, :]

    def sizes(block, chunk):
        part = part_of[chunk]
        start = len(part) * cap + part.index(chunk) * META
        meta = arrays[block, part][start : start + META, 0:1].astype(jnp.float32).astype(jnp.int32)
        return meta[1:2, :], meta[2:3, :]

    def score(early, late):
        for late_chunk in chunks:
            late_first = lane < sizes(late, late_chunk)[0]
            best = best_refs[late][late_chunk : late_chunk + 1, :]
            for chunk in chunks if late_chunk in fresh else fresh:
                scores = dot_last(rows_of(early, chunk), rows_of(late, late_chunk))
                first, both = sizes(early, chunk)
                low = jnp.where(late_first, 0, first)
                high = jnp.where(late_first, first, both)
                if early == late:
                    if chunk == late_chunk:
                        high = jnp.minimum(high, lane)
                    else:
                        high = jnp.where((group_pos ^ chunk) < (group_pos ^ late_chunk), high, 0)
                kept = jnp.where((row >= low) & (row < high), scores, -1.0)
                best = jnp.maximum(best, jnp.max(kept, axis=0, keepdims=True))
            best_refs[late][late_chunk : late_chunk + 1, :] = best

    if inner:
        score(OWN, OWN)
        pl.when(core == 1)(lambda: score(SIB, OWN))
    if not outer:
        return
    pl.when(x == 0)(lambda: score(OWN, XN))
    pl.when(x == 1)(lambda: score(XN, OWN))

    @pl.when(y == 0)
    def _():
        score(OWN, YN)
        score(XN, YN)

    @pl.when(y == 1)
    def _():
        score(YN, OWN)
        score(YN, XN)


def split_kernel(own_ref, x_ref, y_ref, *out_refs):
    best = jnp.maximum(own_ref[...], jnp.maximum(x_ref[...], y_ref[...]))
    for s, ref in enumerate(out_refs):
        ref[...] = best[s : s + 1, :]


def restore_kernel(cap, groups, place_ref, *refs):
    parts, out_ref = refs[:groups], refs[groups]
    rows = place_ref.shape[1]
    hop, rank = place_ref[0:1, :], place_ref[1:2, :]
    total = jnp.zeros((16, rows), jnp.float32)
    for s in range(groups):
        value = parts[s][...]
        high = value.astype(jnp.bfloat16)
        rest = value - high.astype(jnp.float32)
        middle = rest.astype(jnp.bfloat16)
        low = rest - middle.astype(jnp.float32)
        stacked = jnp.concatenate(
            [high.astype(jnp.float32), middle.astype(jnp.float32), low]
            + [jnp.zeros((13, cap), jnp.float32)],
            axis=0,
        ).astype(jnp.bfloat16)
        pick = (iota((cap, rows), 0) == jnp.where(hop == s, rank, -1)).astype(jnp.bfloat16)
        total = total + jnp.dot(stacked, pick, preferred_element_type=jnp.float32)
    out_ref[...] = total[0:1, :] + (total[1:2, :] + total[2:3, :])


def blk_of(y, x, core):
    return (y * 2 + x) * 2 + core


def plane_pairs():
    to_x, to_y, to_sib = [], [], []
    for y in range(2):
        for x in range(2):
            for core in range(2):
                me = blk_of(y, x, core)
                to_x.append((blk_of(y, 1 - x, core ^ x ^ y), me))
                to_y.append((blk_of(1 - y, x, core ^ y), me))
            to_sib.append((blk_of(y, x, 0), blk_of(y, x, 1)))
    return to_x, to_y, to_sib


def reverse(pairs):
    return [(b, a) for a, b in pairs]


def after(value, *others):
    return lax.optimization_barrier((value,) + others)[0]


def score_call(cap, old, new, blocks, before, inner=True, outer=True):
    arrays = [blocks[block][part] for block in blocks_used(inner, outer) for part in old + new]
    return pl.pallas_call(
        functools.partial(score_kernel, cap, old, new, inner, outer),
        out_shape=[jax.ShapeDtypeStruct((4, cap), jnp.float32)] * 3,
        in_specs=vmem_specs(len(arrays) + len(before)),
        out_specs=vmem_specs(3),
        compiler_params=pltpu.CompilerParams(vmem_limit_bytes=VMEM_LIMIT),
        cost_estimate=COST,
    )(*arrays, *before)


def paired_shards(codes, row_scale, row_group, row_sub, centroids):
    row_count, width = codes.shape
    groups = lax.axis_size("group")
    cap = 3 * row_count // (2 * groups)
    params = pltpu.CompilerParams(vmem_limit_bytes=VMEM_LIMIT)

    def chunks_shape(count):
        return jax.ShapeDtypeStruct((count * (cap + META), width), jnp.bfloat16)

    *packed, place = pl.pallas_call(
        functools.partial(pack_kernel, cap),
        out_shape=[chunks_shape(1)] * groups + [jax.ShapeDtypeStruct((8, row_count), jnp.int32)],
        in_specs=vmem_specs(4),
        out_specs=vmem_specs(groups + 1),
        compiler_params=params,
    )(
        row_group.reshape(1, row_count),
        row_sub.reshape(1, row_count),
        row_scale.astype(jnp.float32).reshape(1, row_count),
        codes,
    )
    hops = [[(g, g ^ s) for g in range(groups)] for s in range(groups)]
    to_x, to_y, to_sib = plane_pairs()
    own, sib, x_block, y_block = blocks = [{} for _ in range(4)]

    def spread(part, arrived, sib_after=(), x_after=(), y_after=()):
        unit = pl.pallas_call(
            functools.partial(unit_kernel, cap),
            out_shape=chunks_shape(len(part)),
            in_specs=vmem_specs(len(part) + 1),
            out_specs=pl.BlockSpec(memory_space=pltpu.VMEM),
            compiler_params=params,
            cost_estimate=COST,
        )(*arrived, centroids)
        own[part] = unit
        sib[part] = lax.ppermute(after(unit, *sib_after), "blk", to_sib)
        x_block[part] = lax.ppermute(after(unit, *x_after), "blk", to_x)
        y_block[part] = lax.ppermute(after(unit, *y_after), "blk", to_y)

    near, middle, far = (0,), (2, 1), (3,)
    at_two = lax.ppermute(packed[2], "group", hops[2])
    at_one = lax.ppermute(packed[1], "group", hops[1])
    at_three = lax.ppermute(after(packed[3], at_two), "group", hops[3])
    spread(near, [packed[0]])
    best = score_call(cap, (), (near,), blocks, [])
    spread(middle, [at_two, at_one], [sib[near]], [x_block[near]], [y_block[near]])
    spread(far, [after(at_three, *best)])
    best = score_call(cap, (near,), (middle,), blocks, best)
    best = score_call(cap, (near, middle), (far,), blocks, best, outer=False)
    best, for_x, for_y = score_call(cap, (near, middle), (far,), blocks, best, inner=False)
    returned = pl.pallas_call(
        split_kernel,
        out_shape=[jax.ShapeDtypeStruct((1, cap), jnp.float32)] * groups,
        in_specs=vmem_specs(3),
        out_specs=vmem_specs(groups),
        compiler_params=params,
    )(best, lax.ppermute(for_x, "blk", reverse(to_x)), lax.ppermute(for_y, "blk", reverse(to_y)))
    returned = [returned[0]] + [
        lax.ppermute(returned[s], "group", hops[s]) for s in range(1, groups)
    ]
    out = pl.pallas_call(
        functools.partial(restore_kernel, cap, groups),
        out_shape=jax.ShapeDtypeStruct((1, row_count), jnp.float32),
        in_specs=vmem_specs(groups + 1),
        out_specs=pl.BlockSpec(memory_space=pltpu.VMEM),
        compiler_params=params,
    )(place, *returned)
    return out.reshape(row_count)


def compare(best_sim, own_rows, own_order, own_sub, key_rows, key_order, key_sub):
    scores = jnp.einsum("qd,kd->qk", own_rows, key_rows, preferred_element_type=jnp.float32)
    allowed = (
        (key_sub[None, :] == own_sub[:, None])
        & (key_order[None, :] < own_order[:, None])
        & (key_order[None, :] > 0)
    )
    return jnp.maximum(best_sim, jnp.max(jnp.where(allowed, scores, -1.0), axis=1))


def gathered_shards(codes, row_scale, row_group, row_sub, centroids):
    row_count, width = codes.shape
    groups = lax.axis_size("group")
    capacity = 3 * row_count // (2 * groups)
    slot_count = groups * capacity
    cycle_pos = lax.axis_index("blk")
    group_pos = lax.axis_index("group")
    target = row_group[:, 0]
    member = (target[:, None] == jnp.arange(groups, dtype=jnp.int32)[None, :]).astype(jnp.int32)
    slot_rank = jnp.sum((jnp.cumsum(member, axis=0) - 1) * member, axis=1)
    placed = target * capacity + slot_rank
    row_order = (
        (cycle_pos * groups + group_pos) * row_count + jnp.arange(row_count, dtype=jnp.int32) + 1
    )

    def send(values):
        slots = jnp.zeros((slot_count,) + values.shape[1:], values.dtype).at[placed].set(values)
        return lax.all_to_all(
            slots.reshape((groups, capacity) + values.shape[1:]), "group", 0, 0, tiled=True
        )

    part_codes, part_scale = send(codes), send(row_scale)
    part_sub, part_order = send(row_sub), send(row_order)
    picks = (part_sub[..., None] == jnp.arange(centroids.shape[0], dtype=jnp.int32)).astype(
        jnp.bfloat16
    )
    centre = jnp.einsum("gnc,cd->gnd", picks, centroids, preferred_element_type=jnp.float32)
    vectors = centre + part_scale.astype(jnp.float32)[..., None] * part_codes.astype(jnp.float32)
    unit_part = (
        vectors / jnp.sqrt(jnp.sum(vectors * vectors, axis=-1, keepdims=True) + 1e-06)
    ).astype(jnp.bfloat16)
    own_rows = unit_part.reshape(slot_count, width)
    own_order = part_order.reshape(slot_count)
    own_sub = part_sub.reshape(slot_count)
    stacked = tuple(lax.all_gather(a, "blk", axis=0) for a in (own_rows, own_order, own_sub))

    def per_shard(carry, item):
        return compare(carry, own_rows, own_order, own_sub, *item), None

    start_sim = jnp.full((slot_count,), -1.0, jnp.float32)
    best_sim = lax.scan(per_shard, start_sim, stacked)[0]
    returned = lax.all_to_all(best_sim.reshape(groups, capacity), "group", 0, 0, tiled=True)
    return returned.reshape(-1)[placed]


def solution(mesh):
    paired = mesh.shape["blk"] == 8 and mesh.shape["group"] == 4
    return jax.shard_map(
        paired_shards if paired else gathered_shards,
        mesh=mesh,
        in_specs=(
            P(("blk", "group"), None),
            P(("blk", "group")),
            P(("blk", "group"), None),
            P(("blk", "group")),
            P("group", None),
        ),
        out_specs=P(("blk", "group")),
        check_vma=False,
    )
```

```python
import functools

import jax
import jax.numpy as jnp
from jax import lax
from jax.experimental import pallas as pl
from jax.experimental.pallas import tpu as pltpu
from jax.sharding import PartitionSpec as P

META = 8
OWN, SIB, XN, YN = 0, 1, 2, 3
VMEM_LIMIT = 20 * 1024 * 1024
COST = pl.CostEstimate(flops=1, bytes_accessed=1, transcendentals=0)


def dot_last(a, b):
    return lax.dot_general(a, b, (((1,), (1,)), ((), ())), preferred_element_type=jnp.float32)


def iota(shape, dim):
    return lax.broadcasted_iota(jnp.int32, shape, dim)


def as_column(row):
    n = row.shape[1]
    return jnp.sum(jnp.where(iota((n, n), 0) == iota((n, n), 1), row, 0.0), axis=1, keepdims=True)


def vmem_specs(count):
    return [pl.BlockSpec(memory_space=pltpu.VMEM)] * count


def pack_kernel(cap, group_ref, sub_ref, scale_ref, codes_ref, *out_refs):
    chunk_refs, place_ref = out_refs[:-1], out_refs[-1]
    rows, width = codes_ref.shape
    hop = group_ref[...] ^ lax.axis_index("group")
    keys = iota((16, rows), 0)
    member = keys == hop * 2 + sub_ref[...]
    upto = (iota((rows, rows), 0) <= iota((rows, rows), 1)).astype(jnp.bfloat16)
    counts = jnp.dot(member.astype(jnp.bfloat16), upto, preferred_element_type=jnp.float32)
    totals = counts[:, rows - 1 : rows]
    before = jnp.concatenate([jnp.zeros((1, 1), jnp.float32), totals[:-1]], axis=0)
    base = jnp.where(keys % 2 == 1, before, 0.0) - 1.0
    rank = jnp.sum(jnp.where(member, counts + base, 0.0), axis=0, keepdims=True).astype(jnp.int32)
    place_ref[...] = jnp.concatenate([hop, rank] + [jnp.zeros_like(rank)] * 6, axis=0)
    scales = jnp.concatenate(
        [scale_ref[...], jnp.zeros((15, rows), jnp.float32)], axis=0
    ).astype(jnp.bfloat16)
    codes = codes_ref[...]
    for s, ref in enumerate(chunk_refs):
        pick = (iota((cap, rows), 0) == jnp.where(hop == s, rank, -1)).astype(jnp.bfloat16)
        ref[0:cap, :] = jnp.dot(pick, codes, preferred_element_type=jnp.float32).astype(
            jnp.bfloat16
        )
        first = jnp.broadcast_to(totals[2 * s : 2 * s + 1, :], (1, cap))
        both = first + totals[2 * s + 1 : 2 * s + 2, :]
        meta = jnp.concatenate(
            [dot_last(scales, pick)[0:1, :], first, both, jnp.zeros((META - 3, cap), jnp.float32)],
            axis=0,
        )
        ref[cap:, :] = jnp.concatenate(
            [meta, jnp.zeros((META, width - cap), jnp.float32)], axis=1
        ).astype(jnp.bfloat16)


def unit_kernel(cap, *refs):
    chunk_refs, cent_ref, out_ref = refs[:-2], refs[-2], refs[-1]
    count = len(chunk_refs)
    cent = cent_ref[...].astype(jnp.float32)
    for at, ref in enumerate(chunk_refs):
        meta = ref[cap:, 0:cap].astype(jnp.float32)
        scale = as_column(meta[0:1, :])
        first = meta[1:2, 0:1].astype(jnp.int32)
        centre = jnp.where(iota((cap, 1), 0) < first, cent[0:1, :], cent[1:2, :])
        vectors = centre + scale * ref[0:cap, :].astype(jnp.float32)
        norm = jnp.sqrt(jnp.sum(vectors * vectors, axis=1, keepdims=True) + 1e-06)
        out_ref[at * cap : (at + 1) * cap, :] = (vectors * (1.0 / norm)).astype(jnp.bfloat16)
    out_ref[count * cap :, :] = jnp.concatenate(
        [ref[cap:, :].astype(jnp.float32) for ref in chunk_refs], axis=0
    ).astype(jnp.bfloat16)


OWN_PAIRS, SIB_PAIRS, FAR_PAIRS = "own", "sib", "far"


def score_kernel(cap, keys, jobs, *refs):
    arrays = dict(zip(keys, refs))
    part_of = {chunk: part for _, part in keys for chunk in part}
    rest = refs[len(keys) :]
    best_refs = dict(zip((OWN, XN, YN), rest[-3:]))
    blk = lax.axis_index("blk")
    group_pos = lax.axis_index("group")
    core, x, y = blk % 2, (blk // 2) % 2, blk // 4
    row, lane = iota((cap, cap), 0), iota((1, cap), 1)
    for at, block in enumerate((OWN, XN, YN)):
        if len(rest) > 3:
            best_refs[block][...] = rest[at][...]
        else:
            best_refs[block][...] = jnp.full((4, cap), -1.0, jnp.float32)

    def rows_of(block, chunk):
        part = part_of[chunk]
        start = part.index(chunk) * cap
        return arrays[block, part][start : start + cap, :]

    def sizes(block, chunk):
        part = part_of[chunk]
        meta = arrays[block, part][len(part) * cap :, 0:1].astype(jnp.float32).astype(jnp.int32)
        at = part.index(chunk) * META
        return meta[at + 1 : at + 2, :], meta[at + 2 : at + 3, :]

    def score(early, late, old, new):
        chunks, fresh = sum(old + new, ()), sum(new, ())
        for late_chunk in chunks:
            late_first = lane < sizes(late, late_chunk)[0]
            best = best_refs[late][late_chunk : late_chunk + 1, :]
            for chunk in chunks if late_chunk in fresh else fresh:
                scores = dot_last(rows_of(early, chunk), rows_of(late, late_chunk))
                first, both = sizes(early, chunk)
                low = jnp.where(late_first, 0, first)
                high = jnp.where(late_first, first, both)
                if early == late:
                    if chunk == late_chunk:
                        high = jnp.minimum(high, lane)
                    else:
                        high = jnp.where((group_pos ^ chunk) < (group_pos ^ late_chunk), high, 0)
                kept = jnp.where((row >= low) & (row < high), scores, -1.0)
                best = jnp.maximum(best, jnp.max(kept, axis=0, keepdims=True))
            best_refs[late][late_chunk : late_chunk + 1, :] = best

    for kind, *which in jobs:
        if kind == OWN_PAIRS:
            score(OWN, OWN, *which)
        elif kind == SIB_PAIRS:
            pl.when(core == 1)(functools.partial(score, SIB, OWN, *which))
        else:
            pl.when(x == 0)(functools.partial(score, OWN, XN, *which))
            pl.when(x == 1)(functools.partial(score, XN, OWN, *which))
            pl.when(y == 0)(functools.partial(score, OWN, YN, *which))
            pl.when(y == 0)(functools.partial(score, XN, YN, *which))
            pl.when(y == 1)(functools.partial(score, YN, OWN, *which))
            pl.when(y == 1)(functools.partial(score, YN, XN, *which))


def split_kernel(own_ref, x_ref, y_ref, *out_refs):
    best = jnp.maximum(own_ref[...], jnp.maximum(x_ref[...], y_ref[...]))
    for s, ref in enumerate(out_refs):
        ref[...] = best[s : s + 1, :]


def restore_kernel(cap, groups, place_ref, *refs):
    parts, out_ref = refs[:groups], refs[groups]
    rows = place_ref.shape[1]
    hop, rank = place_ref[0:1, :], place_ref[1:2, :]
    total = jnp.zeros((16, rows), jnp.float32)
    for s in range(groups):
        value = parts[s][...]
        high = value.astype(jnp.bfloat16)
        rest = value - high.astype(jnp.float32)
        middle = rest.astype(jnp.bfloat16)
        low = rest - middle.astype(jnp.float32)
        stacked = jnp.concatenate(
            [high.astype(jnp.float32), middle.astype(jnp.float32), low]
            + [jnp.zeros((13, cap), jnp.float32)],
            axis=0,
        ).astype(jnp.bfloat16)
        pick = (iota((cap, rows), 0) == jnp.where(hop == s, rank, -1)).astype(jnp.bfloat16)
        total = total + jnp.dot(stacked, pick, preferred_element_type=jnp.float32)
    out_ref[...] = total[0:1, :] + (total[1:2, :] + total[2:3, :])


def blk_of(y, x, core):
    return (y * 2 + x) * 2 + core


def plane_pairs():
    to_x, to_y, to_sib = [], [], []
    for y in range(2):
        for x in range(2):
            for core in range(2):
                me = blk_of(y, x, core)
                to_x.append((blk_of(y, 1 - x, core ^ x ^ y), me))
                to_y.append((blk_of(1 - y, x, core ^ y), me))
            to_sib.append((blk_of(y, x, 0), blk_of(y, x, 1)))
    return to_x, to_y, to_sib


def reverse(pairs):
    return [(b, a) for a, b in pairs]


def after(value, *others):
    return lax.optimization_barrier((value,) + others)[0]


def score_call(cap, blocks, jobs, before):
    used = {OWN_PAIRS: (OWN,), SIB_PAIRS: (OWN, SIB), FAR_PAIRS: (OWN, XN, YN)}
    keys = [
        (block, part) for kind, old, new in jobs for block in used[kind] for part in old + new
    ]
    keys = list(dict.fromkeys(keys))
    return pl.pallas_call(
        functools.partial(score_kernel, cap, keys, jobs),
        out_shape=[jax.ShapeDtypeStruct((4, cap), jnp.float32)] * 3,
        in_specs=vmem_specs(len(keys) + len(before)),
        out_specs=vmem_specs(3),
        compiler_params=pltpu.CompilerParams(vmem_limit_bytes=VMEM_LIMIT),
        cost_estimate=COST,
    )(*[blocks[block][part] for block, part in keys], *before)


def paired_shards(codes, row_scale, row_group, row_sub, centroids):
    row_count, width = codes.shape
    groups = lax.axis_size("group")
    cap = 3 * row_count // (2 * groups)
    params = pltpu.CompilerParams(vmem_limit_bytes=VMEM_LIMIT)

    def chunks_shape(count):
        return jax.ShapeDtypeStruct((count * (cap + META), width), jnp.bfloat16)

    *packed, place = pl.pallas_call(
        functools.partial(pack_kernel, cap),
        out_shape=[chunks_shape(1)] * groups + [jax.ShapeDtypeStruct((8, row_count), jnp.int32)],
        in_specs=vmem_specs(4),
        out_specs=vmem_specs(groups + 1),
        compiler_params=params,
    )(
        row_group.reshape(1, row_count),
        row_sub.reshape(1, row_count),
        row_scale.astype(jnp.float32).reshape(1, row_count),
        codes,
    )
    hops = [[(g, g ^ s) for g in range(groups)] for s in range(groups)]
    to_x, to_y, to_sib = plane_pairs()
    own, sib, x_block, y_block = blocks = [{} for _ in range(4)]

    def unit_rows(*arrived):
        return pl.pallas_call(
            functools.partial(unit_kernel, cap),
            out_shape=chunks_shape(len(arrived)),
            in_specs=vmem_specs(len(arrived) + 1),
            out_specs=pl.BlockSpec(memory_space=pltpu.VMEM),
            compiler_params=params,
            cost_estimate=COST,
        )(*arrived, centroids)

    def spread(part, unit, sib_after=(), x_after=(), y_after=()):
        own[part] = unit
        sib[part] = lax.ppermute(after(unit, *sib_after), "blk", to_sib)
        x_block[part] = lax.ppermute(after(unit, *x_after), "blk", to_x)
        y_block[part] = lax.ppermute(after(unit, *y_after), "blk", to_y)

    def score(before, *jobs):
        return score_call(cap, blocks, jobs, before)

    near, middle, far = (0,), (2, 1), (3,)
    at_two = lax.ppermute(packed[2], "group", hops[2])
    at_one = lax.ppermute(packed[1], "group", hops[1])
    at_three = lax.ppermute(after(packed[3], at_two), "group", hops[3])
    spread(near, unit_rows(packed[0]))
    landed = [sib[near], x_block[near], y_block[near]]
    spread(
        middle,
        unit_rows(at_two, at_one),
        landed,
        [x_block[near]],
        [y_block[near]],
    )
    best = score([], (FAR_PAIRS, (), (near,)), (OWN_PAIRS, (), (near, middle)))
    spread(far, unit_rows(after(at_three, *best)), [sib[middle]], [sib[middle]], [sib[middle]])
    best = score(
        best, (FAR_PAIRS, (near,), (middle,)), (SIB_PAIRS, (), (near, middle))
    )
    best = score(best, (OWN_PAIRS, (near, middle), (far,)), (SIB_PAIRS, (near, middle), (far,)))
    best, for_x, for_y = score(best, (FAR_PAIRS, (near, middle), (far,)))
    returned = pl.pallas_call(
        split_kernel,
        out_shape=[jax.ShapeDtypeStruct((1, cap), jnp.float32)] * groups,
        in_specs=vmem_specs(3),
        out_specs=vmem_specs(groups),
        compiler_params=params,
    )(best, lax.ppermute(for_x, "blk", reverse(to_x)), lax.ppermute(for_y, "blk", reverse(to_y)))
    returned = [returned[0]] + [
        lax.ppermute(returned[s], "group", hops[s]) for s in range(1, groups)
    ]
    out = pl.pallas_call(
        functools.partial(restore_kernel, cap, groups),
        out_shape=jax.ShapeDtypeStruct((1, row_count), jnp.float32),
        in_specs=vmem_specs(groups + 1),
        out_specs=pl.BlockSpec(memory_space=pltpu.VMEM),
        compiler_params=params,
    )(place, *returned)
    return out.reshape(row_count)


def compare(best_sim, own_rows, own_order, own_sub, key_rows, key_order, key_sub):
    scores = jnp.einsum("qd,kd->qk", own_rows, key_rows, preferred_element_type=jnp.float32)
    allowed = (
        (key_sub[None, :] == own_sub[:, None])
        & (key_order[None, :] < own_order[:, None])
        & (key_order[None, :] > 0)
    )
    return jnp.maximum(best_sim, jnp.max(jnp.where(allowed, scores, -1.0), axis=1))


def gathered_shards(codes, row_scale, row_group, row_sub, centroids):
    row_count, width = codes.shape
    groups = lax.axis_size("group")
    capacity = 3 * row_count // (2 * groups)
    slot_count = groups * capacity
    cycle_pos = lax.axis_index("blk")
    group_pos = lax.axis_index("group")
    target = row_group[:, 0]
    member = (target[:, None] == jnp.arange(groups, dtype=jnp.int32)[None, :]).astype(jnp.int32)
    slot_rank = jnp.sum((jnp.cumsum(member, axis=0) - 1) * member, axis=1)
    placed = target * capacity + slot_rank
    row_order = (
        (cycle_pos * groups + group_pos) * row_count + jnp.arange(row_count, dtype=jnp.int32) + 1
    )

    def send(values):
        slots = jnp.zeros((slot_count,) + values.shape[1:], values.dtype).at[placed].set(values)
        return lax.all_to_all(
            slots.reshape((groups, capacity) + values.shape[1:]), "group", 0, 0, tiled=True
        )

    part_codes, part_scale = send(codes), send(row_scale)
    part_sub, part_order = send(row_sub), send(row_order)
    picks = (part_sub[..., None] == jnp.arange(centroids.shape[0], dtype=jnp.int32)).astype(
        jnp.bfloat16
    )
    centre = jnp.einsum("gnc,cd->gnd", picks, centroids, preferred_element_type=jnp.float32)
    vectors = centre + part_scale.astype(jnp.float32)[..., None] * part_codes.astype(jnp.float32)
    unit_part = (
        vectors / jnp.sqrt(jnp.sum(vectors * vectors, axis=-1, keepdims=True) + 1e-06)
    ).astype(jnp.bfloat16)
    own_rows = unit_part.reshape(slot_count, width)
    own_order = part_order.reshape(slot_count)
    own_sub = part_sub.reshape(slot_count)
    stacked = tuple(lax.all_gather(a, "blk", axis=0) for a in (own_rows, own_order, own_sub))

    def per_shard(carry, item):
        return compare(carry, own_rows, own_order, own_sub, *item), None

    start_sim = jnp.full((slot_count,), -1.0, jnp.float32)
    best_sim = lax.scan(per_shard, start_sim, stacked)[0]
    returned = lax.all_to_all(best_sim.reshape(groups, capacity), "group", 0, 0, tiled=True)
    return returned.reshape(-1)[placed]


def solution(mesh):
    paired = mesh.shape["blk"] == 8 and mesh.shape["group"] == 4
    return jax.shard_map(
        paired_shards if paired else gathered_shards,
        mesh=mesh,
        in_specs=(
            P(("blk", "group"), None),
            P(("blk", "group")),
            P(("blk", "group"), None),
            P(("blk", "group")),
            P("group", None),
        ),
        out_specs=P(("blk", "group")),
        check_vma=False,
    )
```

```python
import functools

import jax
import jax.numpy as jnp
from jax import lax
from jax.experimental import pallas as pl
from jax.experimental.pallas import tpu as pltpu
from jax.sharding import PartitionSpec as P

META = 8
OWN, SIB, XN, YN = 0, 1, 2, 3
VMEM_LIMIT = 20 * 1024 * 1024
COST = pl.CostEstimate(flops=1, bytes_accessed=1, transcendentals=0)


def dot_last(a, b):
    return lax.dot_general(a, b, (((1,), (1,)), ((), ())), preferred_element_type=jnp.float32)


def iota(shape, dim):
    return lax.broadcasted_iota(jnp.int32, shape, dim)


def as_column(row):
    n = row.shape[1]
    return jnp.sum(jnp.where(iota((n, n), 0) == iota((n, n), 1), row, 0.0), axis=1, keepdims=True)


def vmem_specs(count):
    return [pl.BlockSpec(memory_space=pltpu.VMEM)] * count


def pack_kernel(cap, group_ref, sub_ref, scale_ref, codes_ref, *out_refs):
    chunk_refs, place_ref = out_refs[:-1], out_refs[-1]
    rows, width = codes_ref.shape
    hop = group_ref[...] ^ lax.axis_index("group")
    keys = iota((16, rows), 0)
    member = keys == hop * 2 + sub_ref[...]
    upto = (iota((rows, rows), 0) <= iota((rows, rows), 1)).astype(jnp.bfloat16)
    counts = jnp.dot(member.astype(jnp.bfloat16), upto, preferred_element_type=jnp.float32)
    totals = counts[:, rows - 1 : rows]
    before = jnp.concatenate([jnp.zeros((1, 1), jnp.float32), totals[:-1]], axis=0)
    base = jnp.where(keys % 2 == 1, before, 0.0) - 1.0
    rank = jnp.sum(jnp.where(member, counts + base, 0.0), axis=0, keepdims=True).astype(jnp.int32)
    place_ref[...] = jnp.concatenate([hop, rank] + [jnp.zeros_like(rank)] * 6, axis=0)
    scales = jnp.concatenate(
        [scale_ref[...], jnp.zeros((15, rows), jnp.float32)], axis=0
    ).astype(jnp.bfloat16)
    codes = codes_ref[...]
    for s, ref in enumerate(chunk_refs):
        pick = (iota((cap, rows), 0) == jnp.where(hop == s, rank, -1)).astype(jnp.bfloat16)
        ref[0:cap, :] = jnp.dot(pick, codes, preferred_element_type=jnp.float32).astype(
            jnp.bfloat16
        )
        first = jnp.broadcast_to(totals[2 * s : 2 * s + 1, :], (1, cap))
        both = first + totals[2 * s + 1 : 2 * s + 2, :]
        meta = jnp.concatenate(
            [dot_last(scales, pick)[0:1, :], first, both, jnp.zeros((META - 3, cap), jnp.float32)],
            axis=0,
        )
        ref[cap:, :] = jnp.concatenate(
            [meta, jnp.zeros((META, width - cap), jnp.float32)], axis=1
        ).astype(jnp.bfloat16)


def unit_kernel(cap, *refs):
    chunk_refs, cent_ref, out_ref = refs[:-2], refs[-2], refs[-1]
    count = len(chunk_refs)
    cent = cent_ref[...].astype(jnp.float32)
    for at, ref in enumerate(chunk_refs):
        meta = ref[cap:, 0:cap].astype(jnp.float32)
        scale = as_column(meta[0:1, :])
        first = meta[1:2, 0:1].astype(jnp.int32)
        centre = jnp.where(iota((cap, 1), 0) < first, cent[0:1, :], cent[1:2, :])
        vectors = centre + scale * ref[0:cap, :].astype(jnp.float32)
        norm = jnp.sqrt(jnp.sum(vectors * vectors, axis=1, keepdims=True) + 1e-06)
        out_ref[at * cap : (at + 1) * cap, :] = (vectors * (1.0 / norm)).astype(jnp.bfloat16)
    out_ref[count * cap :, :] = jnp.concatenate(
        [ref[cap:, :].astype(jnp.float32) for ref in chunk_refs], axis=0
    ).astype(jnp.bfloat16)


OWN_PAIRS, SIB_PAIRS, FAR_PAIRS = "own", "sib", "far"


def score_kernel(cap, keys, jobs, *refs):
    arrays = dict(zip(keys, refs))
    part_of = {chunk: part for _, part in keys for chunk in part}
    rest = refs[len(keys) :]
    best_refs = dict(zip((OWN, XN, YN), rest[-3:]))
    blk = lax.axis_index("blk")
    group_pos = lax.axis_index("group")
    core, x, y = blk % 2, (blk // 2) % 2, blk // 4
    row, lane = iota((cap, cap), 0), iota((1, cap), 1)
    for at, block in enumerate((OWN, XN, YN)):
        if len(rest) > 3:
            best_refs[block][...] = rest[at][...]
        else:
            best_refs[block][...] = jnp.full((4, cap), -1.0, jnp.float32)

    def rows_of(block, chunk):
        part = part_of[chunk]
        start = part.index(chunk) * cap
        return arrays[block, part][start : start + cap, :]

    def sizes(block, chunk):
        part = part_of[chunk]
        meta = arrays[block, part][len(part) * cap :, 0:1].astype(jnp.float32).astype(jnp.int32)
        at = part.index(chunk) * META
        return meta[at + 1 : at + 2, :], meta[at + 2 : at + 3, :]

    def score(early, late, old, new):
        chunks, fresh = sum(old + new, ()), sum(new, ())
        for late_chunk in chunks:
            late_first = lane < sizes(late, late_chunk)[0]
            best = best_refs[late][late_chunk : late_chunk + 1, :]
            for chunk in chunks if late_chunk in fresh else fresh:
                scores = dot_last(rows_of(early, chunk), rows_of(late, late_chunk))
                first, both = sizes(early, chunk)
                if early == late:
                    low = jnp.where(late_first, 0, first)
                    high = jnp.where(late_first, first, both)
                    if chunk == late_chunk:
                        high = jnp.minimum(high, lane)
                    else:
                        high = jnp.where((group_pos ^ chunk) < (group_pos ^ late_chunk), high, 0)
                    allowed = (row >= low) & (row < high)
                else:
                    column = iota((cap, 1), 0)
                    code = jnp.where(column < first, 0, jnp.where(column < both, 1, 2))
                    allowed = code == jnp.where(late_first, 0, 1)
                kept = jnp.where(allowed, scores, -1.0)
                best = jnp.maximum(best, jnp.max(kept, axis=0, keepdims=True))
            best_refs[late][late_chunk : late_chunk + 1, :] = best

    for kind, *which in jobs:
        if kind == OWN_PAIRS:
            score(OWN, OWN, *which)
        elif kind == SIB_PAIRS:
            pl.when(core == 1)(functools.partial(score, SIB, OWN, *which))
        else:
            pl.when(x == 0)(functools.partial(score, OWN, XN, *which))
            pl.when(x == 1)(functools.partial(score, XN, OWN, *which))
            pl.when(y == 0)(functools.partial(score, OWN, YN, *which))
            pl.when(y == 0)(functools.partial(score, XN, YN, *which))
            pl.when(y == 1)(functools.partial(score, YN, OWN, *which))
            pl.when(y == 1)(functools.partial(score, YN, XN, *which))


def split_kernel(own_ref, x_ref, y_ref, *out_refs):
    best = jnp.maximum(own_ref[...], jnp.maximum(x_ref[...], y_ref[...]))
    for s, ref in enumerate(out_refs):
        ref[...] = best[s : s + 1, :]


def restore_kernel(cap, groups, place_ref, *refs):
    parts, out_ref = refs[:groups], refs[groups]
    rows = place_ref.shape[1]
    hop, rank = place_ref[0:1, :], place_ref[1:2, :]
    total = jnp.zeros((16, rows), jnp.float32)
    for s in range(groups):
        value = parts[s][...]
        high = value.astype(jnp.bfloat16)
        rest = value - high.astype(jnp.float32)
        middle = rest.astype(jnp.bfloat16)
        low = rest - middle.astype(jnp.float32)
        stacked = jnp.concatenate(
            [high.astype(jnp.float32), middle.astype(jnp.float32), low]
            + [jnp.zeros((13, cap), jnp.float32)],
            axis=0,
        ).astype(jnp.bfloat16)
        pick = (iota((cap, rows), 0) == jnp.where(hop == s, rank, -1)).astype(jnp.bfloat16)
        total = total + jnp.dot(stacked, pick, preferred_element_type=jnp.float32)
    out_ref[...] = total[0:1, :] + (total[1:2, :] + total[2:3, :])


def blk_of(y, x, core):
    return (y * 2 + x) * 2 + core


def plane_pairs():
    to_x, to_y, to_sib = [], [], []
    for y in range(2):
        for x in range(2):
            for core in range(2):
                me = blk_of(y, x, core)
                to_x.append((blk_of(y, 1 - x, core ^ x ^ y), me))
                to_y.append((blk_of(1 - y, x, core ^ y), me))
            to_sib.append((blk_of(y, x, 0), blk_of(y, x, 1)))
    return to_x, to_y, to_sib


def reverse(pairs):
    return [(b, a) for a, b in pairs]


def after(value, *others):
    return lax.optimization_barrier((value,) + others)[0]


def score_call(cap, blocks, jobs, before):
    used = {OWN_PAIRS: (OWN,), SIB_PAIRS: (OWN, SIB), FAR_PAIRS: (OWN, XN, YN)}
    keys = [
        (block, part) for kind, old, new in jobs for block in used[kind] for part in old + new
    ]
    keys = list(dict.fromkeys(keys))
    return pl.pallas_call(
        functools.partial(score_kernel, cap, keys, jobs),
        out_shape=[jax.ShapeDtypeStruct((4, cap), jnp.float32)] * 3,
        in_specs=vmem_specs(len(keys) + len(before)),
        out_specs=vmem_specs(3),
        compiler_params=pltpu.CompilerParams(vmem_limit_bytes=VMEM_LIMIT),
        cost_estimate=COST,
    )(*[blocks[block][part] for block, part in keys], *before)


def paired_shards(codes, row_scale, row_group, row_sub, centroids):
    row_count, width = codes.shape
    groups = lax.axis_size("group")
    cap = 3 * row_count // (2 * groups)
    params = pltpu.CompilerParams(vmem_limit_bytes=VMEM_LIMIT)

    def chunks_shape(count):
        return jax.ShapeDtypeStruct((count * (cap + META), width), jnp.bfloat16)

    *packed, place = pl.pallas_call(
        functools.partial(pack_kernel, cap),
        out_shape=[chunks_shape(1)] * groups + [jax.ShapeDtypeStruct((8, row_count), jnp.int32)],
        in_specs=vmem_specs(4),
        out_specs=vmem_specs(groups + 1),
        compiler_params=params,
    )(
        row_group.reshape(1, row_count),
        row_sub.reshape(1, row_count),
        row_scale.astype(jnp.float32).reshape(1, row_count),
        codes,
    )
    hops = [[(g, g ^ s) for g in range(groups)] for s in range(groups)]
    to_x, to_y, to_sib = plane_pairs()
    own, sib, x_block, y_block = blocks = [{} for _ in range(4)]

    def unit_rows(*arrived):
        return pl.pallas_call(
            functools.partial(unit_kernel, cap),
            out_shape=chunks_shape(len(arrived)),
            in_specs=vmem_specs(len(arrived) + 1),
            out_specs=pl.BlockSpec(memory_space=pltpu.VMEM),
            compiler_params=params,
            cost_estimate=COST,
        )(*arrived, centroids)

    def spread(part, unit, sib_after=(), x_after=(), y_after=()):
        own[part] = unit
        sib[part] = lax.ppermute(after(unit, *sib_after), "blk", to_sib)
        x_block[part] = lax.ppermute(after(unit, *x_after), "blk", to_x)
        y_block[part] = lax.ppermute(after(unit, *y_after), "blk", to_y)

    def score(before, *jobs):
        return score_call(cap, blocks, jobs, before)

    near, middle, far = (0,), (2, 1), (3,)
    at_two = lax.ppermute(packed[2], "group", hops[2])
    at_one = lax.ppermute(packed[1], "group", hops[1])
    at_three = lax.ppermute(after(packed[3], at_two), "group", hops[3])
    spread(near, unit_rows(packed[0]))
    landed = [sib[near], x_block[near], y_block[near]]
    spread(
        middle,
        unit_rows(at_two, at_one),
        landed,
        [x_block[near]],
        [y_block[near]],
    )
    best = score([], (FAR_PAIRS, (), (near,)), (OWN_PAIRS, (), (near, middle)))
    spread(far, unit_rows(after(at_three, *best)), [sib[middle]], [sib[middle]], [sib[middle]])
    best = score(
        best, (FAR_PAIRS, (near,), (middle,)), (SIB_PAIRS, (), (near, middle))
    )
    best = score(best, (OWN_PAIRS, (near, middle), (far,)), (SIB_PAIRS, (near, middle), (far,)))
    best, for_x, for_y = score(best, (FAR_PAIRS, (near, middle), (far,)))
    returned = pl.pallas_call(
        split_kernel,
        out_shape=[jax.ShapeDtypeStruct((1, cap), jnp.float32)] * groups,
        in_specs=vmem_specs(3),
        out_specs=vmem_specs(groups),
        compiler_params=params,
    )(best, lax.ppermute(for_x, "blk", reverse(to_x)), lax.ppermute(for_y, "blk", reverse(to_y)))
    returned = [returned[0]] + [
        lax.ppermute(returned[s], "group", hops[s]) for s in range(1, groups)
    ]
    out = pl.pallas_call(
        functools.partial(restore_kernel, cap, groups),
        out_shape=jax.ShapeDtypeStruct((1, row_count), jnp.float32),
        in_specs=vmem_specs(groups + 1),
        out_specs=pl.BlockSpec(memory_space=pltpu.VMEM),
        compiler_params=params,
    )(place, *returned)
    return out.reshape(row_count)


def compare(best_sim, own_rows, own_order, own_sub, key_rows, key_order, key_sub):
    scores = jnp.einsum("qd,kd->qk", own_rows, key_rows, preferred_element_type=jnp.float32)
    allowed = (
        (key_sub[None, :] == own_sub[:, None])
        & (key_order[None, :] < own_order[:, None])
        & (key_order[None, :] > 0)
    )
    return jnp.maximum(best_sim, jnp.max(jnp.where(allowed, scores, -1.0), axis=1))


def gathered_shards(codes, row_scale, row_group, row_sub, centroids):
    row_count, width = codes.shape
    groups = lax.axis_size("group")
    capacity = 3 * row_count // (2 * groups)
    slot_count = groups * capacity
    cycle_pos = lax.axis_index("blk")
    group_pos = lax.axis_index("group")
    target = row_group[:, 0]
    member = (target[:, None] == jnp.arange(groups, dtype=jnp.int32)[None, :]).astype(jnp.int32)
    slot_rank = jnp.sum((jnp.cumsum(member, axis=0) - 1) * member, axis=1)
    placed = target * capacity + slot_rank
    row_order = (
        (cycle_pos * groups + group_pos) * row_count + jnp.arange(row_count, dtype=jnp.int32) + 1
    )

    def send(values):
        slots = jnp.zeros((slot_count,) + values.shape[1:], values.dtype).at[placed].set(values)
        return lax.all_to_all(
            slots.reshape((groups, capacity) + values.shape[1:]), "group", 0, 0, tiled=True
        )

    part_codes, part_scale = send(codes), send(row_scale)
    part_sub, part_order = send(row_sub), send(row_order)
    picks = (part_sub[..., None] == jnp.arange(centroids.shape[0], dtype=jnp.int32)).astype(
        jnp.bfloat16
    )
    centre = jnp.einsum("gnc,cd->gnd", picks, centroids, preferred_element_type=jnp.float32)
    vectors = centre + part_scale.astype(jnp.float32)[..., None] * part_codes.astype(jnp.float32)
    unit_part = (
        vectors / jnp.sqrt(jnp.sum(vectors * vectors, axis=-1, keepdims=True) + 1e-06)
    ).astype(jnp.bfloat16)
    own_rows = unit_part.reshape(slot_count, width)
    own_order = part_order.reshape(slot_count)
    own_sub = part_sub.reshape(slot_count)
    stacked = tuple(lax.all_gather(a, "blk", axis=0) for a in (own_rows, own_order, own_sub))

    def per_shard(carry, item):
        return compare(carry, own_rows, own_order, own_sub, *item), None

    start_sim = jnp.full((slot_count,), -1.0, jnp.float32)
    best_sim = lax.scan(per_shard, start_sim, stacked)[0]
    returned = lax.all_to_all(best_sim.reshape(groups, capacity), "group", 0, 0, tiled=True)
    return returned.reshape(-1)[placed]


def solution(mesh):
    paired = mesh.shape["blk"] == 8 and mesh.shape["group"] == 4
    return jax.shard_map(
        paired_shards if paired else gathered_shards,
        mesh=mesh,
        in_specs=(
            P(("blk", "group"), None),
            P(("blk", "group")),
            P(("blk", "group"), None),
            P(("blk", "group")),
            P("group", None),
        ),
        out_specs=P(("blk", "group")),
        check_vma=False,
    )
```

```python
import functools

import jax
import jax.numpy as jnp
from jax import lax
from jax.experimental import pallas as pl
from jax.experimental.pallas import tpu as pltpu
from jax.sharding import PartitionSpec as P

META = 8
OWN, SIB, XN, YN = 0, 1, 2, 3
VMEM_LIMIT = 20 * 1024 * 1024
COST = pl.CostEstimate(flops=1, bytes_accessed=1, transcendentals=0)


def dot_last(a, b):
    return lax.dot_general(a, b, (((1,), (1,)), ((), ())), preferred_element_type=jnp.float32)


def iota(shape, dim):
    return lax.broadcasted_iota(jnp.int32, shape, dim)


def as_column(row):
    n = row.shape[1]
    return jnp.sum(jnp.where(iota((n, n), 0) == iota((n, n), 1), row, 0.0), axis=1, keepdims=True)


def vmem_specs(count):
    return [pl.BlockSpec(memory_space=pltpu.VMEM)] * count


def pack_kernel(cap, group_ref, sub_ref, scale_ref, codes_ref, *out_refs):
    chunk_refs, place_ref = out_refs[:-1], out_refs[-1]
    rows, width = codes_ref.shape
    hop = group_ref[...] ^ lax.axis_index("group")
    keys = iota((16, rows), 0)
    member = keys == hop * 2 + sub_ref[...]
    upto = (iota((rows, rows), 0) <= iota((rows, rows), 1)).astype(jnp.bfloat16)
    counts = jnp.dot(member.astype(jnp.bfloat16), upto, preferred_element_type=jnp.float32)
    totals = counts[:, rows - 1 : rows]
    before = jnp.concatenate([jnp.zeros((1, 1), jnp.float32), totals[:-1]], axis=0)
    base = jnp.where(keys % 2 == 1, before, 0.0) - 1.0
    rank = jnp.sum(jnp.where(member, counts + base, 0.0), axis=0, keepdims=True).astype(jnp.int32)
    place_ref[...] = jnp.concatenate([hop, rank] + [jnp.zeros_like(rank)] * 6, axis=0)
    scales = jnp.concatenate(
        [scale_ref[...], jnp.zeros((15, rows), jnp.float32)], axis=0
    ).astype(jnp.bfloat16)
    codes = codes_ref[...]
    for s, ref in enumerate(chunk_refs):
        pick = (iota((cap, rows), 0) == jnp.where(hop == s, rank, -1)).astype(jnp.bfloat16)
        ref[0:cap, :] = jnp.dot(pick, codes, preferred_element_type=jnp.float32).astype(
            jnp.bfloat16
        )
        first = jnp.broadcast_to(totals[2 * s : 2 * s + 1, :], (1, cap))
        both = first + totals[2 * s + 1 : 2 * s + 2, :]
        meta = jnp.concatenate(
            [dot_last(scales, pick)[0:1, :], first, both, jnp.zeros((META - 3, cap), jnp.float32)],
            axis=0,
        )
        ref[cap:, :] = jnp.concatenate(
            [meta, jnp.zeros((META, width - cap), jnp.float32)], axis=1
        ).astype(jnp.bfloat16)


def unit_kernel(cap, *refs):
    chunk_refs, cent_ref, out_ref = refs[:-2], refs[-2], refs[-1]
    count = len(chunk_refs)
    cent = cent_ref[...].astype(jnp.float32)
    for at, ref in enumerate(chunk_refs):
        meta = ref[cap:, 0:cap].astype(jnp.float32)
        scale = as_column(meta[0:1, :])
        first = meta[1:2, 0:1].astype(jnp.int32)
        centre = jnp.where(iota((cap, 1), 0) < first, cent[0:1, :], cent[1:2, :])
        vectors = centre + scale * ref[0:cap, :].astype(jnp.float32)
        norm = jnp.sqrt(jnp.sum(vectors * vectors, axis=1, keepdims=True) + 1e-06)
        out_ref[at * cap : (at + 1) * cap, :] = (vectors * (1.0 / norm)).astype(jnp.bfloat16)
    out_ref[count * cap :, :] = jnp.concatenate(
        [ref[cap:, :].astype(jnp.float32) for ref in chunk_refs], axis=0
    ).astype(jnp.bfloat16)


OWN_PAIRS, SIB_PAIRS, FAR_PAIRS = "own", "sib", "far"


def score_kernel(cap, keys, jobs, *refs):
    arrays = dict(zip(keys, refs))
    part_of = {chunk: part for _, part in keys for chunk in part}
    rest = refs[len(keys) :]
    best_refs = dict(zip((OWN, XN, YN), rest[-3:]))
    blk = lax.axis_index("blk")
    group_pos = lax.axis_index("group")
    core, x, y = blk % 2, (blk // 2) % 2, blk // 4
    row, lane = iota((cap, cap), 0), iota((1, cap), 1)
    for at, block in enumerate((OWN, XN, YN)):
        if len(rest) > 3:
            best_refs[block][...] = rest[at][...]
        else:
            best_refs[block][...] = jnp.full((4, cap), -1.0, jnp.float32)

    def rows_of(block, chunk):
        part = part_of[chunk]
        start = part.index(chunk) * cap
        return arrays[block, part][start : start + cap, :]

    def sizes(block, chunk):
        part = part_of[chunk]
        meta = arrays[block, part][len(part) * cap :, 0:1].astype(jnp.float32).astype(jnp.int32)
        at = part.index(chunk) * META
        return meta[at + 1 : at + 2, :], meta[at + 2 : at + 3, :]

    def score(early, late, old, new):
        chunks, fresh = sum(old + new, ()), sum(new, ())
        for late_chunk in chunks:
            late_first = lane < sizes(late, late_chunk)[0]
            best = best_refs[late][late_chunk : late_chunk + 1, :]
            for chunk in chunks if late_chunk in fresh else fresh:
                scores = dot_last(rows_of(early, chunk), rows_of(late, late_chunk))
                first, both = sizes(early, chunk)
                low = jnp.where(late_first, 0, first)
                high = jnp.where(late_first, first, both)
                if early == late:
                    if chunk == late_chunk:
                        high = jnp.minimum(high, lane)
                    else:
                        high = jnp.where((group_pos ^ chunk) < (group_pos ^ late_chunk), high, 0)
                if early == late:
                    allowed = (row >= low) & (row < high)
                else:
                    column = iota((cap, 1), 0)
                    code = jnp.where(column < first, 0, jnp.where(column < both, 1, 2))
                    allowed = code == jnp.where(late_first, 0, 1)
                kept = jnp.where(allowed, scores, -1.0)
                best = jnp.maximum(best, jnp.max(kept, axis=0, keepdims=True))
            best_refs[late][late_chunk : late_chunk + 1, :] = best

    for kind, *which in jobs:
        if kind == OWN_PAIRS:
            score(OWN, OWN, *which)
        elif kind == SIB_PAIRS:
            pl.when(core == 1)(functools.partial(score, SIB, OWN, *which))
        else:
            pl.when(x == 0)(functools.partial(score, OWN, XN, *which))
            pl.when(x == 1)(functools.partial(score, XN, OWN, *which))
            pl.when(y == 0)(functools.partial(score, OWN, YN, *which))
            pl.when(y == 0)(functools.partial(score, XN, YN, *which))
            pl.when(y == 1)(functools.partial(score, YN, OWN, *which))
            pl.when(y == 1)(functools.partial(score, YN, XN, *which))


def split_kernel(own_ref, x_ref, y_ref, *out_refs):
    best = jnp.maximum(own_ref[...], jnp.maximum(x_ref[...], y_ref[...]))
    for s, ref in enumerate(out_refs):
        ref[...] = best[s : s + 1, :]


def picks_kernel(cap, groups, place_ref, out_ref):
    hop, rank = place_ref[0:1, :], place_ref[1:2, :]
    for s in range(groups):
        pick = iota((cap, hop.shape[1]), 0) == jnp.where(hop == s, rank, -1)
        out_ref[s * cap : (s + 1) * cap, :] = pick.astype(jnp.bfloat16)


def restore_kernel(cap, groups, picks_ref, *refs):
    parts, out_ref = refs[:groups], refs[groups]
    total = jnp.zeros((16, picks_ref.shape[1]), jnp.float32)
    for s in range(groups):
        value = parts[s][...]
        high = value.astype(jnp.bfloat16)
        rest = value - high.astype(jnp.float32)
        middle = rest.astype(jnp.bfloat16)
        low = rest - middle.astype(jnp.float32)
        stacked = jnp.concatenate(
            [high.astype(jnp.float32), middle.astype(jnp.float32), low]
            + [jnp.zeros((13, cap), jnp.float32)],
            axis=0,
        ).astype(jnp.bfloat16)
        pick = picks_ref[s * cap : (s + 1) * cap, :]
        total = total + jnp.dot(stacked, pick, preferred_element_type=jnp.float32)
    out_ref[...] = total[0:1, :] + (total[1:2, :] + total[2:3, :])


def blk_of(y, x, core):
    return (y * 2 + x) * 2 + core


def plane_pairs():
    to_x, to_y, to_sib = [], [], []
    for y in range(2):
        for x in range(2):
            for core in range(2):
                me = blk_of(y, x, core)
                to_x.append((blk_of(y, 1 - x, core ^ x ^ y), me))
                to_y.append((blk_of(1 - y, x, core ^ y), me))
            to_sib.append((blk_of(y, x, 0), blk_of(y, x, 1)))
    return to_x, to_y, to_sib


def reverse(pairs):
    return [(b, a) for a, b in pairs]


def after(value, *others):
    return lax.optimization_barrier((value,) + others)[0]


def score_call(cap, blocks, jobs, before):
    used = {OWN_PAIRS: (OWN,), SIB_PAIRS: (OWN, SIB), FAR_PAIRS: (OWN, XN, YN)}
    keys = [
        (block, part) for kind, old, new in jobs for block in used[kind] for part in old + new
    ]
    keys = list(dict.fromkeys(keys))
    return pl.pallas_call(
        functools.partial(score_kernel, cap, keys, jobs),
        out_shape=[jax.ShapeDtypeStruct((4, cap), jnp.float32)] * 3,
        in_specs=vmem_specs(len(keys) + len(before)),
        out_specs=vmem_specs(3),
        compiler_params=pltpu.CompilerParams(vmem_limit_bytes=VMEM_LIMIT),
        cost_estimate=COST,
    )(*[blocks[block][part] for block, part in keys], *before)


def paired_shards(codes, row_scale, row_group, row_sub, centroids):
    row_count, width = codes.shape
    groups = lax.axis_size("group")
    cap = 3 * row_count // (2 * groups)
    params = pltpu.CompilerParams(vmem_limit_bytes=VMEM_LIMIT)

    def chunks_shape(count):
        return jax.ShapeDtypeStruct((count * (cap + META), width), jnp.bfloat16)

    *packed, place = pl.pallas_call(
        functools.partial(pack_kernel, cap),
        out_shape=[chunks_shape(1)] * groups + [jax.ShapeDtypeStruct((8, row_count), jnp.int32)],
        in_specs=vmem_specs(4),
        out_specs=vmem_specs(groups + 1),
        compiler_params=params,
    )(
        row_group.reshape(1, row_count),
        row_sub.reshape(1, row_count),
        row_scale.astype(jnp.float32).reshape(1, row_count),
        codes,
    )
    hops = [[(g, g ^ s) for g in range(groups)] for s in range(groups)]
    to_x, to_y, to_sib = plane_pairs()
    own, sib, x_block, y_block = blocks = [{} for _ in range(4)]

    def unit_rows(*arrived):
        return pl.pallas_call(
            functools.partial(unit_kernel, cap),
            out_shape=chunks_shape(len(arrived)),
            in_specs=vmem_specs(len(arrived) + 1),
            out_specs=pl.BlockSpec(memory_space=pltpu.VMEM),
            compiler_params=params,
            cost_estimate=COST,
        )(*arrived, centroids)

    def spread(part, unit, sib_after=(), x_after=(), y_after=()):
        own[part] = unit
        sib[part] = lax.ppermute(after(unit, *sib_after), "blk", to_sib)
        x_block[part] = lax.ppermute(after(unit, *x_after), "blk", to_x)
        y_block[part] = lax.ppermute(after(unit, *y_after), "blk", to_y)

    def score(before, *jobs):
        return score_call(cap, blocks, jobs, before)

    near, middle, far = (0,), (2, 1), (3,)
    at_two = lax.ppermute(packed[2], "group", hops[2])
    at_one = lax.ppermute(packed[1], "group", hops[1])
    at_three = lax.ppermute(after(packed[3], at_two), "group", hops[3])
    spread(near, unit_rows(packed[0]))
    landed = [sib[near], x_block[near], y_block[near]]
    spread(
        middle,
        unit_rows(at_two, at_one),
        landed,
        [x_block[near]],
        [y_block[near]],
    )
    picks = pl.pallas_call(
        functools.partial(picks_kernel, cap, groups),
        out_shape=jax.ShapeDtypeStruct((groups * cap, row_count), jnp.bfloat16),
        in_specs=vmem_specs(1),
        out_specs=pl.BlockSpec(memory_space=pltpu.VMEM),
        compiler_params=params,
        cost_estimate=COST,
    )(place)
    own[near] = after(own[near], picks)
    best = score([], (FAR_PAIRS, (), (near,)), (OWN_PAIRS, (), (near, middle)))
    spread(far, unit_rows(after(at_three, *best)), [sib[middle]], [sib[middle]], [sib[middle]])
    best = score(
        best, (FAR_PAIRS, (near,), (middle,)), (SIB_PAIRS, (), (near, middle))
    )
    best = score(best, (OWN_PAIRS, (near, middle), (far,)), (SIB_PAIRS, (near, middle), (far,)))
    best, for_x, for_y = score(best, (FAR_PAIRS, (near, middle), (far,)))
    returned = pl.pallas_call(
        split_kernel,
        out_shape=[jax.ShapeDtypeStruct((1, cap), jnp.float32)] * groups,
        in_specs=vmem_specs(3),
        out_specs=vmem_specs(groups),
        compiler_params=params,
    )(best, lax.ppermute(for_x, "blk", reverse(to_x)), lax.ppermute(for_y, "blk", reverse(to_y)))
    returned = [returned[0]] + [
        lax.ppermute(returned[s], "group", hops[s]) for s in range(1, groups)
    ]
    out = pl.pallas_call(
        functools.partial(restore_kernel, cap, groups),
        out_shape=jax.ShapeDtypeStruct((1, row_count), jnp.float32),
        in_specs=vmem_specs(groups + 1),
        out_specs=pl.BlockSpec(memory_space=pltpu.VMEM),
        compiler_params=params,
    )(picks, *returned)
    return out.reshape(row_count)


def compare(best_sim, own_rows, own_order, own_sub, key_rows, key_order, key_sub):
    scores = jnp.einsum("qd,kd->qk", own_rows, key_rows, preferred_element_type=jnp.float32)
    allowed = (
        (key_sub[None, :] == own_sub[:, None])
        & (key_order[None, :] < own_order[:, None])
        & (key_order[None, :] > 0)
    )
    return jnp.maximum(best_sim, jnp.max(jnp.where(allowed, scores, -1.0), axis=1))


def gathered_shards(codes, row_scale, row_group, row_sub, centroids):
    row_count, width = codes.shape
    groups = lax.axis_size("group")
    capacity = 3 * row_count // (2 * groups)
    slot_count = groups * capacity
    cycle_pos = lax.axis_index("blk")
    group_pos = lax.axis_index("group")
    target = row_group[:, 0]
    member = (target[:, None] == jnp.arange(groups, dtype=jnp.int32)[None, :]).astype(jnp.int32)
    slot_rank = jnp.sum((jnp.cumsum(member, axis=0) - 1) * member, axis=1)
    placed = target * capacity + slot_rank
    row_order = (
        (cycle_pos * groups + group_pos) * row_count + jnp.arange(row_count, dtype=jnp.int32) + 1
    )

    def send(values):
        slots = jnp.zeros((slot_count,) + values.shape[1:], values.dtype).at[placed].set(values)
        return lax.all_to_all(
            slots.reshape((groups, capacity) + values.shape[1:]), "group", 0, 0, tiled=True
        )

    part_codes, part_scale = send(codes), send(row_scale)
    part_sub, part_order = send(row_sub), send(row_order)
    picks = (part_sub[..., None] == jnp.arange(centroids.shape[0], dtype=jnp.int32)).astype(
        jnp.bfloat16
    )
    centre = jnp.einsum("gnc,cd->gnd", picks, centroids, preferred_element_type=jnp.float32)
    vectors = centre + part_scale.astype(jnp.float32)[..., None] * part_codes.astype(jnp.float32)
    unit_part = (
        vectors / jnp.sqrt(jnp.sum(vectors * vectors, axis=-1, keepdims=True) + 1e-06)
    ).astype(jnp.bfloat16)
    own_rows = unit_part.reshape(slot_count, width)
    own_order = part_order.reshape(slot_count)
    own_sub = part_sub.reshape(slot_count)
    stacked = tuple(lax.all_gather(a, "blk", axis=0) for a in (own_rows, own_order, own_sub))

    def per_shard(carry, item):
        return compare(carry, own_rows, own_order, own_sub, *item), None

    start_sim = jnp.full((slot_count,), -1.0, jnp.float32)
    best_sim = lax.scan(per_shard, start_sim, stacked)[0]
    returned = lax.all_to_all(best_sim.reshape(groups, capacity), "group", 0, 0, tiled=True)
    return returned.reshape(-1)[placed]


def solution(mesh):
    paired = mesh.shape["blk"] == 8 and mesh.shape["group"] == 4
    return jax.shard_map(
        paired_shards if paired else gathered_shards,
        mesh=mesh,
        in_specs=(
            P(("blk", "group"), None),
            P(("blk", "group")),
            P(("blk", "group"), None),
            P(("blk", "group")),
            P("group", None),
        ),
        out_specs=P(("blk", "group")),
        check_vma=False,
    )
```
